32 devices in a mesh: front: 4 (over z), lat: 8 (over y, x, core).
Axes of the slice: x: 2, y: 2, z: 4, core: 2. Of those that a mesh axis runs over, the one named last changes fastest.
Arguments:
- samples: float32 [64, 128, 128], P('front', 'lat'), may hold values from -6 to 6
- reaction: float32 [64, 128], P('front', 'lat'), may hold values from 0.5 to 2
- weight_x: float32 [64, 128], P('front', 'lat'), may hold values from 0.2 to 1
- weight_y: float32 [64, 128], P('front', 'lat'), may hold values from 0.2 to 1
- inverses: float32 [4, 16, 128, 128], P('front', 'lat'), may hold values from -0.3 to 0.4
- couplings: float32 [4, 16, 128, 128], P('front', 'lat'), may hold values from -12 to 12
Outputs:
- whitened: float32 [64, 128, 128], P('front', 'lat')
- gradients: float32 [3, 64, 128], P(None, 'front', 'lat')
The draws below stay inside these ranges and needn't reach their ends.
All inputs are finite; a program needn't handle non-finite values.
Results may differ from the reference program's by a relative error of at most 0.0003.
Values sent between devices are 32-bit elements; how exact they have to be, the bound alone decides.
A program may use at most 192 MiB of HBM per device.

```python
import math
import jax
import jax.numpy as jnp
from jax import lax

W = 128
P_SIZE = 2
TX = 16
R = 128
TY = 16
GX = 64
GY = 128
BLOCKS = 64
N_FRONT = 4
N_LAT = 8


def factor_blocks(key):
    grand_accumulation = N_FRONT * N_LAT * P_SIZE
    half = W // 2
    scales = jax.random.uniform(jax.random.fold_in(key, 11), (grand_accumulation, W), jnp.float32, 0.15, 0.4)
    lower = jnp.clip(jax.random.normal(jax.random.fold_in(key, 12), (grand_accumulation, half, half), jnp.float32) * 0.125, -0.6, 0.6)
    exclusive_bound = jnp.zeros((grand_accumulation, W, W), jnp.float32).at[:, half:, :half].set(lower)
    rate = jnp.exp(jax.random.uniform(jax.random.fold_in(key, 13), (W,), jnp.float32, math.log(1.0 / grand_accumulation), math.log(1.0 / 30.0)))
    factor = jax.random.uniform(jax.random.fold_in(key, 14), (grand_accumulation,), jnp.float32, 0.6, 1.5)
    keep_indicator = 1.0 - rate[None, :] * factor[:, None]
    batch_shift = jax.random.randint(jax.random.fold_in(key, 15), (3,), 0, grand_accumulation)
    batch_cluster = jnp.any(jnp.arange(grand_accumulation)[:, None] == batch_shift[None, :], axis=1)
    keep_indicator = keep_indicator * jnp.where(batch_cluster, 0.8, 1.0)[:, None]
    eye = jnp.eye(W, dtype=jnp.float32)
    noise = jax.random.normal(jax.random.fold_in(key, 16), (grand_accumulation, W, W), jnp.float32) * 0.003
    mixing = noise + eye[None, :, :] * keep_indicator[:, :, None]
    inverse = (eye[None, :, :] + exclusive_bound) * scales[:, None, :]
    product = mixing - jnp.einsum('kij,kjl->kil', exclusive_bound, mixing, precision=lax.Precision.HIGHEST)
    coupling = -(1.0 / scales)[:, :, None] * product
    return (inverse.reshape(N_FRONT, N_LAT * P_SIZE, W, W), coupling.reshape(N_FRONT, N_LAT * P_SIZE, W, W))


def draw_inverses(key, part):
    return factor_blocks(key)[0]


def draw_couplings(key, part):
    return factor_blocks(key)[1]


def level_of(rng, extent, split, low, top_value):
    loudness = 1.0
    for axis_at, blocks in split:
        heights = jax.random.uniform(jax.random.fold_in(jax.random.fold_in(rng, 6), axis_at), (blocks,), jnp.float32, low / len(split), top_value / len(split))
        loudness = loudness * jnp.repeat(jnp.exp(heights), extent[axis_at] // blocks).reshape((-1,) + (1,) * (len(extent) - 1 - axis_at))
    return loudness


def centred(own_key, extent, deviation, limit, cuts=(), kind=jnp.bfloat16):
    values = deviation * jax.random.normal(own_key, extent, jnp.float32)
    if cuts:
        values = values * level_of(own_key, extent, cuts, -0.22, 0.18)
    return jnp.clip(values, -limit, limit).astype(kind)


def setup_inputs(seed: int = 0) -> dict:
    key_of = jax.random.split(jax.random.key(seed), 7)
    samples = centred(key_of[0], (GX, GY, R), 1.0, 6.0, ((0, 4), (1, 8)), jnp.float32)
    reaction = jnp.clip(jnp.exp(math.log(2.0) - 1.3862944 * jax.random.uniform(key_of[1], (GX, GY), jnp.float32) ** level_of(key_of[1], (GX, GY), ((0, 4), (1, 8)), -0.2, 0.2)), 0.5, 2.0)
    weight_x = jnp.clip(jnp.exp(math.log(1.0) - 1.609438 * jax.random.uniform(key_of[2], (GX, GY), jnp.float32) ** level_of(key_of[2], (GX, GY), ((0, 4), (1, 8)), -0.2, 0.2)), 0.2, 1.0)
    weight_y = jnp.clip(jnp.exp(math.log(1.0) - 1.609438 * jax.random.uniform(key_of[3], (GX, GY), jnp.float32) ** level_of(key_of[3], (GX, GY), ((0, 4), (1, 8)), -0.2, 0.2)), 0.2, 1.0)
    inverses = draw_inverses(jax.random.fold_in(key_of[6], 71), 0)
    couplings = draw_couplings(jax.random.fold_in(key_of[6], 71), 0)
    return dict(samples=samples, reaction=reaction, weight_x=weight_x, weight_y=weight_y, inverses=inverses, couplings=couplings)


def matmul(left, right):
    return jnp.dot(left, right, precision=lax.Precision.HIGHEST, preferred_element_type=jnp.float32)


def to_blocks(field):
    return field.reshape(N_FRONT, TX, N_LAT, TY, R).transpose(0, 2, 1, 3, 4).reshape(BLOCKS, W, R)


def from_blocks(blocks):
    return blocks.reshape(N_FRONT, N_LAT, TX, TY, R).transpose(0, 2, 1, 3, 4).reshape(GX, GY, R)


def reference(samples, reaction, weight_x, weight_y, inverses, couplings):
    padded = jnp.pad(samples, ((1, 1), (1, 1), (0, 0)))
    lap_x = 2.0 * samples - padded[:-2, 1:-1] - padded[2:, 1:-1]
    lap_y = 2.0 * samples - padded[1:-1, :-2] - padded[1:-1, 2:]
    resid = reaction[:, :, None] * samples + weight_x[:, :, None] * lap_x + weight_y[:, :, None] * lap_y
    blocks = to_blocks(resid)
    reciprocal_pieces = inverses.reshape(BLOCKS, W, W)
    lower_band_coupling = couplings.reshape(BLOCKS, W, W)

    def forward(running_carry, element_list):
        inverse_k, coupling_k, rhs_k = element_list
        result = matmul(inverse_k, rhs_k - matmul(coupling_k, running_carry))
        return result, result

    initial_carry = jnp.zeros((W, R), jnp.float32)
    unused_value, unknown_answer = lax.scan(forward, initial_carry, (reciprocal_pieces, lower_band_coupling, blocks))

    def upward_substitution(running_carry, element_list):
        inverse_k, coupling_k, solved_k = element_list
        result = matmul(inverse_k.T, solved_k - running_carry)
        return matmul(coupling_k.T, result), result

    unused_value, reverse_mode_pieces = lax.scan(upward_substitution, initial_carry, (reciprocal_pieces, lower_band_coupling, unknown_answer), reverse=True)
    whitened = from_blocks(reverse_mode_pieces)
    gradients = jnp.stack([jnp.mean(whitened * samples, axis=2), jnp.mean(whitened * lap_x, axis=2), jnp.mean(whitened * lap_y, axis=2)])
    return whitened, gradients
```

```python
import functools
import jax
import jax.numpy as jnp
from jax import lax
from jax.experimental import pallas as pl
from jax.experimental.pallas import tpu as pltpu
from jax.sharding import PartitionSpec as P

MESH = pl.DeviceIdType.MESH
F32 = jnp.float32
BF16 = jnp.bfloat16


def split(value):
    high = value.astype(BF16)
    return high, (value - high.astype(F32)).astype(BF16)


def product(left, right, transposed=False):
    dim = 0 if transposed else 1
    lh, ll = split(left)
    rh, rl = split(right)
    return lax.dot_general(
        jnp.concatenate([lh, ll, lh], axis=dim),
        jnp.concatenate([rh, rh, rl], axis=0),
        (((dim,), (0,)), ((), ())),
        preferred_element_type=F32,
    )


def pair(left, right):
    return jnp.concatenate([left, right], axis=1)


def kernel(n_front, n_lat, samples, reaction, weight_x, weight_y, inverses, couplings,
           white, grad, lap_x, lap_y, edges, halo_x, halo_y, maps, values, right_map, left_map,
           total, recv, halo_send, halo_recv, sends, recvs):
    front, lat = lax.axis_index("front"), lax.axis_index("lat")
    lat_rounds = n_lat.bit_length() - 1
    rounds = lat_rounds + n_front.bit_length() - 1
    tx, ty, count = samples.shape
    w = inverses.shape[-1]

    def bit_of(r):
        if r < lat_rounds:
            return lax.rem(lax.div(lat, 1 << r), 2)
        return lax.rem(lax.div(front, 1 << (r - lat_rounds)), 2)

    def partner(r):
        sign = 1 - 2 * bit_of(r)
        if r < lat_rounds:
            return (front, lat + sign * (1 << r))
        return (front + sign * (1 << (r - lat_rounds)), lat)

    neighbours = (
        (front < n_front - 1, (front + 1, lat)),
        (front > 0, (front - 1, lat)),
        (lat < n_lat - 1, (front, lat + 1)),
        (lat > 0, (front, lat - 1)),
    )

    barrier = pltpu.get_barrier_semaphore()
    for r in range(rounds):
        pl.semaphore_signal(barrier, inc=1, device_id=partner(r), device_id_type=MESH)
    for exists, target in neighbours:
        @pl.when(exists)
        def _(target=target):
            pl.semaphore_signal(barrier, inc=1, device_id=target, device_id_type=MESH)

    s = samples[...]
    edges[0] = s[:, ty - 1, :]
    edges[1] = s[:, 0, :]
    inv0, inv1 = inverses[0, 0], inverses[0, 1]
    t0 = -product(inv0, couplings[0, 0])
    t1 = -product(inv1, couplings[0, 1])
    maps[0] = t0
    maps[2] = t1

    peers = rounds
    for exists, _ in neighbours:
        peers = peers + exists.astype(jnp.int32)
    pl.semaphore_wait(barrier, peers)

    halos = []
    for i, (source, landing) in enumerate((
        (samples.at[tx - 1], halo_x.at[0]),
        (samples.at[0], halo_x.at[1]),
        (edges.at[0], halo_y.at[0]),
        (edges.at[1], halo_y.at[1]),
    )):
        halos.append(pltpu.make_async_remote_copy(
            src_ref=source, dst_ref=landing, send_sem=halo_send.at[i], recv_sem=halo_recv.at[i],
            device_id=neighbours[i][1], device_id_type=MESH))

        @pl.when(neighbours[i][0])
        def _(i=i):
            halos[i].start()

    full = product(t1, t0)
    maps[1] = full
    stack = maps[0:2].reshape(2 * w, w)
    total[0, 0] = full
    for i, landing in enumerate((halo_x.at[0], halo_x.at[1], halo_y.at[0], halo_y.at[1])):
        comes = neighbours[i ^ 1][0]

        @pl.when(comes)
        def _(i=i):
            halos[i].wait_recv()

        @pl.when(jnp.logical_not(comes))
        def _(landing=landing):
            landing[...] = jnp.zeros((landing.shape[0], count), F32)

    hx, hy = halo_x[...], halo_y[...]
    lx = 2.0 * s - jnp.concatenate([hx[0:1], s[:-1]], 0) - jnp.concatenate([s[1:], hx[1:2]], 0)
    ly = 2.0 * s - jnp.concatenate([hy[0][:, None, :], s[:, :-1]], 1) - jnp.concatenate([s[:, 1:], hy[1][:, None, :]], 1)
    lap_x[...] = lx
    lap_y[...] = ly
    resid = (reaction[...][:, :, None] * s + weight_x[...][:, :, None] * lx
             + weight_y[...][:, :, None] * ly).reshape(2 * w, count)
    y0 = product(inv0, resid[:w])
    y1 = product(inv1, resid[w:]) + product(t1, y0)
    values[0] = y0
    values[1] = y1
    total[0, 1] = y1
    adj = -product(stack, pair(stack, jnp.concatenate([y0, y1], 0)), True)
    total[0, 2] = adj[:, :w]
    total[0, 3] = adj[:, w:]

    def copy(r, part):
        if r == rounds - 1 and part == 0:
            window = pl.ds(1, 1)
        else:
            window = pl.ds(2 * part, 2)
        return pltpu.make_async_remote_copy(
            src_ref=total.at[r, window], dst_ref=recv.at[r, window],
            send_sem=sends.at[r, part], recv_sem=recvs.at[r, part],
            device_id=partner(r), device_id_type=MESH)

    def send(r, part):
        if r < rounds - 1:
            copy(r, part).start()
        else:
            @pl.when(bit_of(r) == part)
            def _():
                copy(r, part).start()

    send(0, 0)
    send(0, 1)
    eye = (lax.broadcasted_iota(jnp.int32, (w, w), 0) == lax.broadcasted_iota(jnp.int32, (w, w), 1)).astype(F32)
    zero = jnp.zeros((w, w), F32)
    left_map[0] = eye
    left_map[1] = zero
    right_map[0] = eye
    right_map[1] = zero
    right_map[2] = zero
    right_map[3] = zero

    def joined(earlier, later, store):
        start = earlier(0)
        ab = pair(start, earlier(1))
        new = product(later(0), ab)
        store(0, new[:, :w], new[:, w:] + later(1))
        mid = product(later(2), ab)
        mid = pair(mid[:, :w], mid[:, w:] + later(3))
        new = product(start, mid, True)
        store(1, earlier(2) + new[:, :w], earlier(3) + new[:, w:])

    for r in range(rounds - 1):
        copy(r, 0).wait_recv()
        copy(r, 1).wait_recv()

        def store_total(part, first, second, r=r):
            total[r + 1, 2 * part] = first
            total[r + 1, 2 * part + 1] = second
            send(r + 1, part)

        def store_right(part, first, second):
            right_map[2 * part] = first
            right_map[2 * part + 1] = second

        mine = lambda i, r=r: total[r, i]
        other = lambda i, r=r: recv[r, i]

        @pl.when(bit_of(r) == 0)
        def _():
            joined(mine, other, store_total)
            joined(lambda i: right_map[i], other, store_right)

        @pl.when(bit_of(r) == 1)
        def _():
            joined(other, mine, store_total)
            new = product(left_map[0], pair(other(0), other(1)))
            left_map[0] = new[:, :w]
            left_map[1] = new[:, w:] + left_map[1]

    r = rounds - 1

    @pl.when(bit_of(r) == 0)
    def _():
        copy(r, 1).wait_recv()
        middle = product(recv[r, 2], total[r, 1]) + recv[r, 3]
        right_map[3] = right_map[3] + product(right_map[0], middle, True)

    @pl.when(bit_of(r) == 1)
    def _():
        copy(r, 0).wait_recv()
        left_map[1] = product(left_map[0], recv[r, 1]) + left_map[1]

    y = values[...].reshape(2 * w, count) + product(maps[0:2].reshape(2 * w, w), left_map[1])
    c = product(right_map[2], y[w:]) + right_map[3]
    both = product(pair(inverses[0, 1], maps[2]), y[w:] - c, True)
    x0 = product(inverses[0, 0], y[:w] + both[w:], True)
    out = jnp.concatenate([x0, both[:w]], 0).reshape(tx, ty, count)
    white[...] = out
    grad[0] = jnp.sum(out * samples[...], axis=2) * (1.0 / count)
    grad[1] = jnp.sum(out * lap_x[...], axis=2) * (1.0 / count)
    grad[2] = jnp.sum(out * lap_y[...], axis=2) * (1.0 / count)

    for i in range(4):
        @pl.when(neighbours[i][0])
        def _(i=i):
            halos[i].wait_send()
    for r in range(rounds - 1):
        copy(r, 0).wait_send()
        copy(r, 1).wait_send()
    for part in range(2):
        @pl.when(bit_of(rounds - 1) == part)
        def _(part=part):
            copy(rounds - 1, part).wait_send()


def body(n_front, n_lat, samples, reaction, weight_x, weight_y, inverses, couplings):
    tx, ty, count = samples.shape
    w = inverses.shape[-1]
    rounds = n_lat.bit_length() + n_front.bit_length() - 2
    vmem = pl.BlockSpec(memory_space=pltpu.VMEM)
    return pl.pallas_call(
        functools.partial(kernel, n_front, n_lat),
        out_shape=(jax.ShapeDtypeStruct((tx, ty, count), F32), jax.ShapeDtypeStruct((3, tx, ty), F32)),
        in_specs=[vmem] * 6,
        out_specs=(vmem, vmem),
        scratch_shapes=[
            pltpu.VMEM((tx, ty, count), F32),
            pltpu.VMEM((tx, ty, count), F32),
            pltpu.VMEM((2, tx, count), F32),
            pltpu.VMEM((2, ty, count), F32),
            pltpu.VMEM((2, tx, count), F32),
            pltpu.VMEM((3, w, w), F32),
            pltpu.VMEM((2, w, count), F32),
            pltpu.VMEM((4, w, w), F32),
            pltpu.VMEM((2, w, w), F32),
            pltpu.VMEM((rounds, 4, w, w), F32),
            pltpu.VMEM((rounds, 4, w, w), F32),
            pltpu.SemaphoreType.DMA((4,)),
            pltpu.SemaphoreType.DMA((4,)),
            pltpu.SemaphoreType.DMA((rounds, 2)),
            pltpu.SemaphoreType.DMA((rounds, 2)),
        ],
        compiler_params=pltpu.CompilerParams(
            collective_id=0, has_side_effects=True, vmem_limit_bytes=48 * 1024 * 1024),
    )(samples, reaction, weight_x, weight_y, inverses, couplings)


def solution(mesh):
    placed = (
        P("front", "lat", None),
        P("front", "lat"),
        P("front", "lat"),
        P("front", "lat"),
        P("front", "lat", None, None),
        P("front", "lat", None, None),
    )
    return jax.shard_map(
        functools.partial(body, mesh.shape["front"], mesh.shape["lat"]),
        mesh=mesh,
        in_specs=placed,
        out_specs=(P("front", "lat", None), P(None, "front", "lat")),
        check_vma=False,
    )
```

```python
import functools
import jax
import jax.numpy as jnp
from jax import lax
from jax.experimental import pallas as pl
from jax.experimental.pallas import tpu as pltpu
from jax.sharding import PartitionSpec as P

MESH = pl.DeviceIdType.MESH
F32 = jnp.float32
BF16 = jnp.bfloat16


def split(value):
    high = value.astype(BF16)
    return high, (value - high.astype(F32)).astype(BF16)


def product(left, right, transposed=False):
    dim = 0 if transposed else 1
    lh, ll = split(left)
    rh, rl = split(right)
    return lax.dot_general(
        jnp.concatenate([lh, ll, lh], axis=dim),
        jnp.concatenate([rh, rh, rl], axis=0),
        (((dim,), (0,)), ((), ())),
        preferred_element_type=F32,
    )


def pair(left, right):
    return jnp.concatenate([left, right], axis=1)


def kernel(n_front, n_lat, samples_in, reaction_in, weight_x_in, weight_y_in, inverses_in, couplings_in,
           white, grad, samples, reaction, weight_x, weight_y, inverses, couplings, loads, lap_x, lap_y, edges, halo_x, halo_y, maps, values, right_map, left_map,
           total, recv, halo_send, halo_recv, sends, recvs):
    front, lat = lax.axis_index("front"), lax.axis_index("lat")
    lat_rounds = n_lat.bit_length() - 1
    rounds = lat_rounds + n_front.bit_length() - 1
    tx, ty, count = samples.shape
    w = inverses.shape[-1]

    def bit_of(r):
        if r < lat_rounds:
            return lax.rem(lax.div(lat, 1 << r), 2)
        return lax.rem(lax.div(front, 1 << (r - lat_rounds)), 2)

    def partner(r):
        sign = 1 - 2 * bit_of(r)
        if r < lat_rounds:
            return (front, lat + sign * (1 << r))
        return (front + sign * (1 << (r - lat_rounds)), lat)

    neighbours = (
        (front < n_front - 1, (front + 1, lat)),
        (front > 0, (front - 1, lat)),
        (lat < n_lat - 1, (front, lat + 1)),
        (lat > 0, (front, lat - 1)),
    )

    inputs = [
        pltpu.make_async_copy(source, here, loads.at[i]) for i, (source, here) in enumerate((
            (samples_in, samples), (reaction_in, reaction), (weight_x_in, weight_x),
            (weight_y_in, weight_y), (inverses_in, inverses), (couplings_in, couplings)))]
    for i in (0, 4, 5, 1, 2, 3):
        inputs[i].start()
    barrier = pltpu.get_barrier_semaphore()
    for r in range(rounds):
        pl.semaphore_signal(barrier, inc=1, device_id=partner(r), device_id_type=MESH)
    for exists, target in neighbours:
        @pl.when(exists)
        def _(target=target):
            pl.semaphore_signal(barrier, inc=1, device_id=target, device_id_type=MESH)

    samples_copy, reaction_copy, weight_x_copy, weight_y_copy, inverses_copy, couplings_copy = inputs
    samples_copy.wait()
    s = samples[...]
    edges[0] = s[:, ty - 1, :]
    edges[1] = s[:, 0, :]
    inverses_copy.wait()
    couplings_copy.wait()
    inv0, inv1 = inverses[0, 0], inverses[0, 1]
    t0 = -product(inv0, couplings[0, 0])
    t1 = -product(inv1, couplings[0, 1])
    maps[0] = t0
    maps[2] = t1

    peers = rounds
    for exists, _ in neighbours:
        peers = peers + exists.astype(jnp.int32)
    pl.semaphore_wait(barrier, peers)

    halos = []
    for i, (source, landing) in enumerate((
        (samples.at[tx - 1], halo_x.at[0]),
        (samples.at[0], halo_x.at[1]),
        (edges.at[0], halo_y.at[0]),
        (edges.at[1], halo_y.at[1]),
    )):
        halos.append(pltpu.make_async_remote_copy(
            src_ref=source, dst_ref=landing, send_sem=halo_send.at[i], recv_sem=halo_recv.at[i],
            device_id=neighbours[i][1], device_id_type=MESH))

        @pl.when(neighbours[i][0])
        def _(i=i):
            halos[i].start()

    full = product(t1, t0)
    maps[1] = full
    stack = maps[0:2].reshape(2 * w, w)
    total[0, 0] = full
    for i, landing in enumerate((halo_x.at[0], halo_x.at[1], halo_y.at[0], halo_y.at[1])):
        comes = neighbours[i ^ 1][0]

        @pl.when(comes)
        def _(i=i):
            halos[i].wait_recv()

        @pl.when(jnp.logical_not(comes))
        def _(landing=landing):
            landing[...] = jnp.zeros((landing.shape[0], count), F32)

    reaction_copy.wait()
    weight_x_copy.wait()
    weight_y_copy.wait()
    hx, hy = halo_x[...], halo_y[...]
    lx = 2.0 * s - jnp.concatenate([hx[0:1], s[:-1]], 0) - jnp.concatenate([s[1:], hx[1:2]], 0)
    ly = 2.0 * s - jnp.concatenate([hy[0][:, None, :], s[:, :-1]], 1) - jnp.concatenate([s[:, 1:], hy[1][:, None, :]], 1)
    lap_x[...] = lx
    lap_y[...] = ly
    resid = (reaction[...][:, :, None] * s + weight_x[...][:, :, None] * lx
             + weight_y[...][:, :, None] * ly).reshape(2 * w, count)
    y0 = product(inv0, resid[:w])
    y1 = product(inv1, resid[w:]) + product(t1, y0)
    values[0] = y0
    values[1] = y1
    total[0, 1] = y1
    core = bit_of(0)

    def swap(part):
        window = pl.ds(2 * part, 2)
        return pltpu.make_async_remote_copy(
            src_ref=total.at[0, window], dst_ref=recv.at[0, window],
            send_sem=sends.at[0, part], recv_sem=recvs.at[0, part],
            device_id=partner(0), device_id_type=MESH)

    def piece(ref, r, kind, which):
        if kind == 0:
            return ref.at[r, 1, pl.ds(which * (w // 2), w // 2)]
        if kind == 1:
            return ref.at[r, pl.ds(2 + which, 1)]
        return ref.at[r, pl.ds(2 * which, 2)]

    def direct(r, kind=2, which=core):
        return pltpu.make_async_remote_copy(
            src_ref=piece(total, r, kind, which), dst_ref=piece(recv, r, kind, which),
            send_sem=sends.at[r, 0], recv_sem=recvs.at[r, which],
            device_id=partner(r), device_id_type=MESH)

    def relay(r, kind=2, which=core):
        return pltpu.make_async_remote_copy(
            src_ref=piece(recv, r, kind, which), dst_ref=piece(recv, r, kind, which),
            send_sem=sends.at[r, 1], recv_sem=recvs.at[r, which],
            device_id=partner(0), device_id_type=MESH)

    def receive(r, kind=2):
        direct(r, kind).wait_recv()
        relay(r, kind).start()
        relay(r, kind, 1 - core).wait_recv()

    def send(r, part):
        if r < rounds - 1:
            @pl.when(core == part)
            def _():
                direct(r, which=part).start()
        else:
            @pl.when(bit_of(r) == part)
            def _():
                direct(r, part).start()

    swap(0).start()
    adj = -product(stack, pair(stack, jnp.concatenate([y0, y1], 0)), True)
    total[0, 2] = adj[:, :w]
    total[0, 3] = adj[:, w:]
    swap(1).start()
    eye = (lax.broadcasted_iota(jnp.int32, (w, w), 0) == lax.broadcasted_iota(jnp.int32, (w, w), 1)).astype(F32)
    zero = jnp.zeros((w, w), F32)
    left_map[0] = eye
    left_map[1] = zero
    right_map[0] = eye
    right_map[1] = zero
    right_map[2] = zero
    right_map[3] = zero

    def joined(earlier, later, store):
        start = earlier(0)
        ab = pair(start, earlier(1))
        both = product(jnp.concatenate([later(0), later(2)], 0), ab)
        store(0, both[:w, :w], both[:w, w:] + later(1))
        mid = pair(both[w:, :w], both[w:, w:] + later(3))
        new = product(start, mid, True)
        store(1, earlier(2) + new[:, :w], earlier(3) + new[:, w:])

    for r in range(rounds - 1):
        if r == 0:
            swap(0).wait_recv()
            swap(1).wait_recv()
        else:
            receive(r)

        def store_total(part, first, second, r=r):
            total[r + 1, 2 * part] = first
            total[r + 1, 2 * part + 1] = second
            send(r + 1, part)

        def store_right(part, first, second):
            right_map[2 * part] = first
            right_map[2 * part + 1] = second

        mine = lambda i, r=r: total[r, i]
        other = lambda i, r=r: recv[r, i]

        @pl.when(bit_of(r) == 0)
        def _():
            joined(mine, other, store_total)
            joined(lambda i: right_map[i], other, store_right)

        @pl.when(bit_of(r) == 1)
        def _():
            joined(other, mine, store_total)
            new = product(left_map[0], pair(other(0), other(1)))
            left_map[0] = new[:, :w]
            left_map[1] = new[:, w:] + left_map[1]

    r = rounds - 1

    @pl.when(bit_of(r) == 0)
    def _():
        receive(r, 1)
        middle = product(recv[r, 2], total[r, 1]) + recv[r, 3]
        right_map[3] = right_map[3] + product(right_map[0], middle, True)

    @pl.when(bit_of(r) == 1)
    def _():
        receive(r, 0)
        left_map[1] = product(left_map[0], recv[r, 1]) + left_map[1]

    y = values[...].reshape(2 * w, count) + product(maps[0:2].reshape(2 * w, w), left_map[1])
    c = product(right_map[2], y[w:]) + right_map[3]
    both = product(pair(inverses[0, 1], maps[2]), y[w:] - c, True)
    x0 = product(inverses[0, 0], y[:w] + both[w:], True)
    out = jnp.concatenate([x0, both[:w]], 0).reshape(tx, ty, count)
    white[...] = out
    grad[0] = jnp.sum(out * samples[...], axis=2) * (1.0 / count)
    grad[1] = jnp.sum(out * lap_x[...], axis=2) * (1.0 / count)
    grad[2] = jnp.sum(out * lap_y[...], axis=2) * (1.0 / count)

    for i in range(4):
        @pl.when(neighbours[i][0])
        def _(i=i):
            halos[i].wait_send()
    swap(0).wait_send()
    swap(1).wait_send()
    for r in range(1, rounds - 1):
        direct(r).wait_send()
        relay(r).wait_send()
    for part in range(2):
        @pl.when(bit_of(rounds - 1) == part)
        def _(part=part):
            direct(rounds - 1, part).wait_send()
            relay(rounds - 1, 1 - part).wait_send()


def body(n_front, n_lat, *arrays):
    samples, inverses = arrays[0], arrays[4]
    tx, ty, count = samples.shape
    w = inverses.shape[-1]
    rounds = n_lat.bit_length() + n_front.bit_length() - 2
    vmem = pl.BlockSpec(memory_space=pltpu.VMEM)
    return pl.pallas_call(
        functools.partial(kernel, n_front, n_lat),
        out_shape=(jax.ShapeDtypeStruct((tx, ty, count), F32), jax.ShapeDtypeStruct((3, tx, ty), F32)),
        in_specs=[pl.BlockSpec(memory_space=pltpu.HBM)] * 6,
        out_specs=(vmem, vmem),
        scratch_shapes=[
            *[pltpu.VMEM(a.shape, F32) for a in arrays],
            pltpu.SemaphoreType.DMA((6,)),
            pltpu.VMEM((tx, ty, count), F32),
            pltpu.VMEM((tx, ty, count), F32),
            pltpu.VMEM((2, tx, count), F32),
            pltpu.VMEM((2, ty, count), F32),
            pltpu.VMEM((2, tx, count), F32),
            pltpu.VMEM((3, w, w), F32),
            pltpu.VMEM((2, w, count), F32),
            pltpu.VMEM((4, w, w), F32),
            pltpu.VMEM((2, w, w), F32),
            pltpu.VMEM((rounds, 4, w, w), F32),
            pltpu.VMEM((rounds, 4, w, w), F32),
            pltpu.SemaphoreType.DMA((4,)),
            pltpu.SemaphoreType.DMA((4,)),
            pltpu.SemaphoreType.DMA((rounds, 2)),
            pltpu.SemaphoreType.DMA((rounds, 2)),
        ],
        compiler_params=pltpu.CompilerParams(
            collective_id=0, has_side_effects=True, vmem_limit_bytes=64 * 1024 * 1024 - 128 * 1024),
    )(*arrays)


def solution(mesh):
    placed = (
        P("front", "lat", None),
        P("front", "lat"),
        P("front", "lat"),
        P("front", "lat"),
        P("front", "lat", None, None),
        P("front", "lat", None, None),
    )
    return jax.shard_map(
        functools.partial(body, mesh.shape["front"], mesh.shape["lat"]),
        mesh=mesh,
        in_specs=placed,
        out_specs=(P("front", "lat", None), P(None, "front", "lat")),
        check_vma=False,
    )
```

```python
import functools
import jax
import jax.numpy as jnp
from jax import lax
from jax.experimental import pallas as pl
from jax.experimental.pallas import tpu as pltpu
from jax.sharding import PartitionSpec as P

MESH = pl.DeviceIdType.MESH
F32 = jnp.float32
BF16 = jnp.bfloat16


def split(value):
    high = value.astype(BF16)
    return high, (value - high.astype(F32)).astype(BF16)


def product(left, right, transposed=False):
    dim = 0 if transposed else 1
    lh, ll = split(left)
    rh, rl = split(right)
    return lax.dot_general(
        jnp.concatenate([lh, ll, lh], axis=dim),
        jnp.concatenate([rh, rh, rl], axis=0),
        (((dim,), (0,)), ((), ())),
        preferred_element_type=F32,
    )


def pair(left, right):
    return jnp.concatenate([left, right], axis=1)


def kernel(n_front, n_lat, samples_in, reaction_in, weight_x_in, weight_y_in, inverses_in, couplings_in,
           white, grad, samples, reaction, weight_x, weight_y, inverses, couplings, loads, lap_x, lap_y, edges, halo_x, halo_y, maps, values, right_map, left_map,
           total, recv, halo_send, halo_recv, sends, recvs):
    front, lat = lax.axis_index("front"), lax.axis_index("lat")
    lat_rounds = n_lat.bit_length() - 1
    rounds = lat_rounds + n_front.bit_length() - 1
    tx, ty, count = samples.shape
    w = inverses.shape[-1]

    def bit_of(r):
        if r < lat_rounds:
            return lax.rem(lax.div(lat, 1 << r), 2)
        return lax.rem(lax.div(front, 1 << (r - lat_rounds)), 2)

    def partner(r):
        sign = 1 - 2 * bit_of(r)
        if r < lat_rounds:
            return (front, lat + sign * (1 << r))
        return (front + sign * (1 << (r - lat_rounds)), lat)

    neighbours = (
        (front < n_front - 1, (front + 1, lat)),
        (front > 0, (front - 1, lat)),
        (lat < n_lat - 1, (front, lat + 1)),
        (lat > 0, (front, lat - 1)),
    )

    inputs = [
        pltpu.make_async_copy(source, here, loads.at[i]) for i, (source, here) in enumerate((
            (samples_in, samples), (reaction_in, reaction), (weight_x_in, weight_x),
            (weight_y_in, weight_y), (inverses_in, inverses), (couplings_in, couplings)))]
    for i in (0, 4, 5, 1, 2, 3):
        inputs[i].start()
    barrier = pltpu.get_barrier_semaphore()
    for r in range(rounds):
        pl.semaphore_signal(barrier, inc=1, device_id=partner(r), device_id_type=MESH)
    for exists, target in neighbours:
        @pl.when(exists)
        def _(target=target):
            pl.semaphore_signal(barrier, inc=1, device_id=target, device_id_type=MESH)

    samples_copy, reaction_copy, weight_x_copy, weight_y_copy, inverses_copy, couplings_copy = inputs
    samples_copy.wait()
    s = samples[...]
    edges[0] = s[:, ty - 1, :]
    edges[1] = s[:, 0, :]
    inverses_copy.wait()
    couplings_copy.wait()
    inv0, inv1 = inverses[0, 0], inverses[0, 1]
    t0 = -product(inv0, couplings[0, 0])
    t1 = -product(inv1, couplings[0, 1])
    maps[0] = t0
    maps[2] = t1

    peers = rounds
    for exists, _ in neighbours:
        peers = peers + exists.astype(jnp.int32)
    pl.semaphore_wait(barrier, peers)

    halos = []
    for i, (source, landing) in enumerate((
        (samples.at[tx - 1], halo_x.at[0]),
        (samples.at[0], halo_x.at[1]),
        (edges.at[0], halo_y.at[0]),
        (edges.at[1], halo_y.at[1]),
    )):
        halos.append(pltpu.make_async_remote_copy(
            src_ref=source, dst_ref=landing, send_sem=halo_send.at[i], recv_sem=halo_recv.at[i],
            device_id=neighbours[i][1], device_id_type=MESH))

        @pl.when(neighbours[i][0])
        def _(i=i):
            halos[i].start()

    full = product(t1, t0)
    maps[1] = full
    stack = maps[0:2].reshape(2 * w, w)
    total[0, 0] = full
    for i, landing in enumerate((halo_x.at[0], halo_x.at[1], halo_y.at[0], halo_y.at[1])):
        comes = neighbours[i ^ 1][0]

        @pl.when(comes)
        def _(i=i):
            halos[i].wait_recv()

        @pl.when(jnp.logical_not(comes))
        def _(landing=landing):
            landing[...] = jnp.zeros((landing.shape[0], count), F32)

    reaction_copy.wait()
    weight_x_copy.wait()
    weight_y_copy.wait()
    hx, hy = halo_x[...], halo_y[...]
    lx = 2.0 * s - jnp.concatenate([hx[0:1], s[:-1]], 0) - jnp.concatenate([s[1:], hx[1:2]], 0)
    ly = 2.0 * s - jnp.concatenate([hy[0][:, None, :], s[:, :-1]], 1) - jnp.concatenate([s[:, 1:], hy[1][:, None, :]], 1)
    lap_x[...] = lx
    lap_y[...] = ly
    resid = (reaction[...][:, :, None] * s + weight_x[...][:, :, None] * lx
             + weight_y[...][:, :, None] * ly).reshape(2 * w, count)
    y0 = product(inv0, resid[:w])
    y1 = product(inv1, resid[w:]) + product(t1, y0)
    values[0] = y0
    values[1] = y1
    total[0, 1] = y1
    core = bit_of(0)

    def swap(part):
        window = pl.ds(2 * part, 2)
        return pltpu.make_async_remote_copy(
            src_ref=total.at[0, window], dst_ref=recv.at[0, window],
            send_sem=sends.at[0, part], recv_sem=recvs.at[0, part],
            device_id=partner(0), device_id_type=MESH)

    def piece(ref, r, kind, which):
        if kind == 0:
            return ref.at[r, 1, pl.ds(which * (w // 2), w // 2)]
        if kind == 1:
            return ref.at[r, pl.ds(2 + which, 1)]
        return ref.at[r, pl.ds(2 * which, 2)]

    def remote(source, landing, sent, arrived, target):
        return pltpu.make_async_remote_copy(
            src_ref=source, dst_ref=landing, send_sem=sent, recv_sem=arrived,
            device_id=target, device_id_type=MESH)

    def direct(r, kind, which):
        return remote(piece(total, r, kind, which), piece(recv, r, kind, which),
                      sends.at[r, 0], recvs.at[r, which], partner(r))

    def relay(r, kind, which):
        return remote(piece(recv, r, kind, which), piece(recv, r, kind, which),
                      sends.at[r, 2], recvs.at[r, which], partner(0))

    def receive(r, kind):
        direct(r, kind, core).wait_recv()
        relay(r, kind, core).start()
        relay(r, kind, 1 - core).wait_recv()

    def matrix(side, which, k):
        return which + 2 * k if side == 0 else 2 * which + k

    def give(r, side, k, which=core):
        m = matrix(side, which, k)
        return remote(total.at[r, m], recv.at[r, m], sends.at[r, k], recvs.at[r, m], partner(r))

    def hand(r, side, k, which=core):
        m = matrix(side, which, k)
        return remote(recv.at[r, m], recv.at[r, m], sends.at[r, 2 + k], recvs.at[r, m], partner(0))

    def send(r, part):
        if r < rounds - 1:
            @pl.when(bit_of(r) == 0)
            def _():
                give(r, 0, part).start()

            @pl.when((bit_of(r) == 1) & (core == part))
            def _():
                give(r, 1, 0, part).start()
                give(r, 1, 1, part).start()
        else:
            @pl.when(bit_of(r) == part)
            def _():
                direct(r, part, core).start()

    swap(0).start()
    adj = -product(stack, pair(stack, jnp.concatenate([y0, y1], 0)), True)
    total[0, 2] = adj[:, :w]
    total[0, 3] = adj[:, w:]
    swap(1).start()
    eye = (lax.broadcasted_iota(jnp.int32, (w, w), 0) == lax.broadcasted_iota(jnp.int32, (w, w), 1)).astype(F32)
    zero = jnp.zeros((w, w), F32)
    left_map[0] = eye
    left_map[1] = zero
    right_map[0] = eye
    right_map[1] = zero
    right_map[2] = zero
    right_map[3] = zero

    def joined(earlier, later, store, needs=(None, None, None)):
        wait = lambda i: needs[i]() if needs[i] else None
        start = earlier(0)
        ab = pair(start, earlier(1))
        both = product(jnp.concatenate([later(0), later(2)], 0), ab)
        wait(0)
        store(0, both[:w, :w], both[:w, w:] + later(1))
        wait(1)
        mid = pair(both[w:, :w], both[w:, w:] + later(3))
        new = product(start, mid, True)
        wait(2)
        store(1, earlier(2) + new[:, :w], earlier(3) + new[:, w:])

    for r in range(rounds - 1):
        def store_total(part, first, second, r=r):
            total[r + 1, 2 * part] = first
            total[r + 1, 2 * part + 1] = second
            send(r + 1, part)

        def store_right(part, first, second):
            right_map[2 * part] = first
            right_map[2 * part + 1] = second

        mine = lambda i, r=r: total[r, i]
        other = lambda i, r=r: recv[r, i]

        def arrive(side, k, r=r):
            give(r, side, k).wait_recv()
            hand(r, side, k).start()

        def settle(side, k, r=r):
            hand(r, side, k, 1 - core).wait_recv()

        if r == 0:
            swap(0).wait_recv()
            swap(1).wait_recv()

        @pl.when(bit_of(r) == 0)
        def _():
            def rest():
                arrive(1, 1)
                settle(1, 1)

            if r > 0:
                arrive(1, 0)
                settle(1, 0)
            joined(mine, other, store_total, (rest if r > 0 else None, None, None))
            joined(lambda i: right_map[i], other, store_right)

        @pl.when(bit_of(r) == 1)
        def _():
            if r > 0:
                arrive(0, 0)
                settle(0, 0)
                needs = (None, functools.partial(arrive, 0, 1), functools.partial(settle, 0, 1))
            else:
                needs = (None, None, None)
            joined(other, mine, store_total, needs)
            new = product(left_map[0], pair(other(0), other(1)))
            left_map[0] = new[:, :w]
            left_map[1] = new[:, w:] + left_map[1]

    r = rounds - 1

    @pl.when(bit_of(r) == 0)
    def _():
        receive(r, 1)
        middle = product(recv[r, 2], total[r, 1]) + recv[r, 3]
        right_map[3] = right_map[3] + product(right_map[0], middle, True)

    @pl.when(bit_of(r) == 1)
    def _():
        receive(r, 0)
        left_map[1] = product(left_map[0], recv[r, 1]) + left_map[1]

    y = values[...].reshape(2 * w, count) + product(maps[0:2].reshape(2 * w, w), left_map[1])
    c = product(right_map[2], y[w:]) + right_map[3]
    both = product(pair(inverses[0, 1], maps[2]), y[w:] - c, True)
    x0 = product(inverses[0, 0], y[:w] + both[w:], True)
    out = jnp.concatenate([x0, both[:w]], 0).reshape(tx, ty, count)
    white[...] = out
    grad[0] = jnp.sum(out * samples[...], axis=2) * (1.0 / count)
    grad[1] = jnp.sum(out * lap_x[...], axis=2) * (1.0 / count)
    grad[2] = jnp.sum(out * lap_y[...], axis=2) * (1.0 / count)

    for i in range(4):
        @pl.when(neighbours[i][0])
        def _(i=i):
            halos[i].wait_send()
    swap(0).wait_send()
    swap(1).wait_send()
    for r in range(1, rounds - 1):
        for side in range(2):
            @pl.when(bit_of(r) == side)
            def _(r=r, side=side):
                for k in range(2):
                    give(r, side, k).wait_send()
                    hand(r, 1 - side, k).wait_send()
    for part in range(2):
        @pl.when(bit_of(rounds - 1) == part)
        def _(part=part):
            direct(rounds - 1, part, core).wait_send()
            relay(rounds - 1, 1 - part, core).wait_send()


def body(n_front, n_lat, *arrays):
    samples, inverses = arrays[0], arrays[4]
    tx, ty, count = samples.shape
    w = inverses.shape[-1]
    rounds = n_lat.bit_length() + n_front.bit_length() - 2
    vmem = pl.BlockSpec(memory_space=pltpu.VMEM)
    return pl.pallas_call(
        functools.partial(kernel, n_front, n_lat),
        out_shape=(pltpu.VMEM((tx, ty, count), F32), pltpu.VMEM((3, tx, ty), F32)),
        in_specs=[pl.BlockSpec(memory_space=pltpu.HBM)] * 6,
        out_specs=(vmem, vmem),
        scratch_shapes=[
            *[pltpu.VMEM(a.shape, F32) for a in arrays],
            pltpu.SemaphoreType.DMA((6,)),
            pltpu.VMEM((tx, ty, count), F32),
            pltpu.VMEM((tx, ty, count), F32),
            pltpu.VMEM((2, tx, count), F32),
            pltpu.VMEM((2, ty, count), F32),
            pltpu.VMEM((2, tx, count), F32),
            pltpu.VMEM((3, w, w), F32),
            pltpu.VMEM((2, w, count), F32),
            pltpu.VMEM((4, w, w), F32),
            pltpu.VMEM((2, w, w), F32),
            pltpu.VMEM((rounds, 4, w, w), F32),
            pltpu.VMEM((rounds, 4, w, w), F32),
            pltpu.SemaphoreType.DMA((4,)),
            pltpu.SemaphoreType.DMA((4,)),
            pltpu.SemaphoreType.DMA((rounds, 4)),
            pltpu.SemaphoreType.DMA((rounds, 4)),
        ],
        compiler_params=pltpu.CompilerParams(
            collective_id=0, has_side_effects=True, vmem_limit_bytes=48 * 1024 * 1024),
    )(*[pltpu.with_memory_space_constraint(a, pltpu.HBM) for a in arrays])


def solution(mesh):
    placed = (
        P("front", "lat", None),
        P("front", "lat"),
        P("front", "lat"),
        P("front", "lat"),
        P("front", "lat", None, None),
        P("front", "lat", None, None),
    )
    return jax.shard_map(
        functools.partial(body, mesh.shape["front"], mesh.shape["lat"]),
        mesh=mesh,
        in_specs=placed,
        out_specs=(P("front", "lat", None), P(None, "front", "lat")),
        check_vma=False,
    )
```

```python
import functools
import jax
import jax.numpy as jnp
from jax import lax
from jax.experimental import pallas as pl
from jax.experimental.pallas import tpu as pltpu
from jax.sharding import PartitionSpec as P

MESH = pl.DeviceIdType.MESH
F32 = jnp.float32
BF16 = jnp.bfloat16


def split(value):
    high = value.astype(BF16)
    return high, (value - high.astype(F32)).astype(BF16)


def product(left, right, transposed=False):
    dim = 0 if transposed else 1
    lh, ll = split(left)
    rh, rl = split(right)
    return lax.dot_general(
        jnp.concatenate([lh, ll, lh], axis=dim),
        jnp.concatenate([rh, rh, rl], axis=0),
        (((dim,), (0,)), ((), ())),
        preferred_element_type=F32,
    )


def pair(left, right):
    return jnp.concatenate([left, right], axis=1)


def kernel(n_front, n_lat, samples_in, reaction_in, weight_x_in, weight_y_in, inverses_in, couplings_in,
           white, grad, samples, reaction, weight_x, weight_y, inverses, couplings, loads, lap_x, lap_y, edges, halo_x, halo_y, maps, tails, values, right_map, left_map,
           total, recv, halo_send, halo_recv, sends, recvs):
    front, lat = lax.axis_index("front"), lax.axis_index("lat")
    lat_rounds = n_lat.bit_length() - 1
    rounds = lat_rounds + n_front.bit_length() - 1
    tx, ty, count = samples.shape
    w = inverses.shape[-1]

    def bit_of(r):
        if r < lat_rounds:
            return lax.rem(lax.div(lat, 1 << r), 2)
        return lax.rem(lax.div(front, 1 << (r - lat_rounds)), 2)

    def partner(r):
        sign = 1 - 2 * bit_of(r)
        if r < lat_rounds:
            return (front, lat + sign * (1 << r))
        return (front + sign * (1 << (r - lat_rounds)), lat)

    neighbours = (
        (front < n_front - 1, (front + 1, lat)),
        (front > 0, (front - 1, lat)),
        (lat < n_lat - 1, (front, lat + 1)),
        (lat > 0, (front, lat - 1)),
    )

    inputs = [
        pltpu.make_async_copy(source, here, loads.at[i]) for i, (source, here) in enumerate((
            (samples_in, samples), (reaction_in, reaction), (weight_x_in, weight_x),
            (weight_y_in, weight_y), (inverses_in, inverses), (couplings_in, couplings)))]
    for i in (0, 4, 5, 1, 2, 3):
        inputs[i].start()
    barrier = pltpu.get_barrier_semaphore()
    for r in range(rounds):
        pl.semaphore_signal(barrier, inc=1, device_id=partner(r), device_id_type=MESH)
    for exists, target in neighbours:
        @pl.when(exists)
        def _(target=target):
            pl.semaphore_signal(barrier, inc=1, device_id=target, device_id_type=MESH)

    samples_copy, reaction_copy, weight_x_copy, weight_y_copy, inverses_copy, couplings_copy = inputs
    samples_copy.wait()
    s = samples[...]
    edges[0] = s[:, ty - 1, :]
    edges[1] = s[:, 0, :]
    inverses_copy.wait()
    couplings_copy.wait()
    inv0, inv1 = inverses[0, 0], inverses[0, 1]
    t0 = -product(inv0, couplings[0, 0])
    t1 = -product(inv1, couplings[0, 1])
    maps[0] = t0

    peers = rounds
    for exists, _ in neighbours:
        peers = peers + exists.astype(jnp.int32)
    pl.semaphore_wait(barrier, peers)

    halos = []
    for i, (source, landing) in enumerate((
        (samples.at[tx - 1], halo_x.at[0]),
        (samples.at[0], halo_x.at[1]),
        (edges.at[0], halo_y.at[0]),
        (edges.at[1], halo_y.at[1]),
    )):
        halos.append(pltpu.make_async_remote_copy(
            src_ref=source, dst_ref=landing, send_sem=halo_send.at[i], recv_sem=halo_recv.at[i],
            device_id=neighbours[i][1], device_id_type=MESH))

        @pl.when(neighbours[i][0])
        def _(i=i):
            halos[i].start()

    full = product(t1, t0)
    maps[1] = full
    stack = maps[0:2].reshape(2 * w, w)
    total[0, 0] = full
    tail = product(t1, inv0)
    tails[0] = inv1
    tails[1] = tail
    total[0, 2] = -product(stack, stack, True)
    for i, landing in enumerate((halo_x.at[0], halo_x.at[1], halo_y.at[0], halo_y.at[1])):
        comes = neighbours[i ^ 1][0]

        @pl.when(comes)
        def _(i=i):
            halos[i].wait_recv()

        @pl.when(jnp.logical_not(comes))
        def _(landing=landing):
            landing[...] = jnp.zeros((landing.shape[0], count), F32)

    reaction_copy.wait()
    weight_x_copy.wait()
    weight_y_copy.wait()
    hx, hy = halo_x[...], halo_y[...]
    lx = 2.0 * s - jnp.concatenate([hx[0:1], s[:-1]], 0) - jnp.concatenate([s[1:], hx[1:2]], 0)
    ly = 2.0 * s - jnp.concatenate([hy[0][:, None, :], s[:, :-1]], 1) - jnp.concatenate([s[:, 1:], hy[1][:, None, :]], 1)
    lap_x[...] = lx
    lap_y[...] = ly
    resid = (reaction[...][:, :, None] * s + weight_x[...][:, :, None] * lx
             + weight_y[...][:, :, None] * ly).reshape(2 * w, count)
    y0 = product(inv0, resid[:w])
    y1 = product(pair(tail, inv1), resid)
    values[0] = y0
    values[1] = y1
    total[0, 1] = y1
    core = bit_of(0)

    def swap(part):
        window = pl.ds(2 * part, 2)
        return pltpu.make_async_remote_copy(
            src_ref=total.at[0, window], dst_ref=recv.at[0, window],
            send_sem=sends.at[0, part], recv_sem=recvs.at[0, part],
            device_id=partner(0), device_id_type=MESH)

    def piece(ref, r, kind, which):
        if kind == 0:
            return ref.at[r, 1, pl.ds(which * (w // 2), w // 2)]
        if kind == 1:
            return ref.at[r, pl.ds(2 + which, 1)]
        return ref.at[r, pl.ds(2 * which, 2)]

    def remote(source, landing, sent, arrived, target):
        return pltpu.make_async_remote_copy(
            src_ref=source, dst_ref=landing, send_sem=sent, recv_sem=arrived,
            device_id=target, device_id_type=MESH)

    def direct(r, kind, which):
        return remote(piece(total, r, kind, which), piece(recv, r, kind, which),
                      sends.at[r, 0], recvs.at[r, which], partner(r))

    def relay(r, kind, which):
        return remote(piece(recv, r, kind, which), piece(recv, r, kind, which),
                      sends.at[r, 2], recvs.at[r, which], partner(0))

    def receive(r, kind):
        direct(r, kind, core).wait_recv()
        relay(r, kind, core).start()
        relay(r, kind, 1 - core).wait_recv()

    def matrix(side, which, k):
        return which + 2 * k if side == 0 else 2 * which + k

    def give(r, side, k, which=core):
        m = matrix(side, which, k)
        return remote(total.at[r, m], recv.at[r, m], sends.at[r, k], recvs.at[r, m], partner(r))

    def hand(r, side, k, which=core):
        m = matrix(side, which, k)
        return remote(recv.at[r, m], recv.at[r, m], sends.at[r, 2 + k], recvs.at[r, m], partner(0))

    def send(r, part):
        if r < rounds - 1:
            @pl.when(bit_of(r) == 0)
            def _():
                give(r, 0, part).start()

            @pl.when((bit_of(r) == 1) & (core == part))
            def _():
                give(r, 1, 0, part).start()
                give(r, 1, 1, part).start()
        else:
            @pl.when(bit_of(r) == part)
            def _():
                direct(r, part, core).start()

    swap(0).start()
    total[0, 3] = -product(stack, jnp.concatenate([y0, y1], 0), True)
    swap(1).start()
    eye = (lax.broadcasted_iota(jnp.int32, (w, w), 0) == lax.broadcasted_iota(jnp.int32, (w, w), 1)).astype(F32)
    zero = jnp.zeros((w, w), F32)
    def joined(earlier, later, store, needs=(None, None, None)):
        wait = lambda i: needs[i]() if needs[i] else None
        start = earlier(0)
        ab = pair(start, earlier(1))
        both = product(jnp.concatenate([later(0), later(2)], 0), ab)
        wait(0)
        store(0, both[:w, :w], both[:w, w:] + later(1))
        wait(1)
        mid = pair(both[w:, :w], both[w:, w:] + later(3))
        new = product(start, mid, True)
        wait(2)
        store(1, earlier(2) + new[:, :w], earlier(3) + new[:, w:])

    for r in range(rounds - 1):
        def store_total(part, first, second, r=r):
            total[r + 1, 2 * part] = first
            total[r + 1, 2 * part + 1] = second
            send(r + 1, part)

        def store_right(part, first, second):
            right_map[2 * part] = first
            right_map[2 * part + 1] = second

        mine = lambda i, r=r: total[r, i]
        other = lambda i, r=r: recv[r, i]

        def arrive(side, k, r=r):
            give(r, side, k).wait_recv()
            hand(r, side, k).start()

        def settle(side, k, r=r):
            hand(r, side, k, 1 - core).wait_recv()

        if r == 0:
            swap(0).wait_recv()
            swap(1).wait_recv()

        @pl.when(bit_of(r) == 0)
        def _():
            def rest():
                arrive(1, 1)
                settle(1, 1)

            if r > 0:
                arrive(1, 0)
                settle(1, 0)
            joined(mine, other, store_total, (rest if r > 0 else None, None, None))
            if r > 0:
                joined(lambda i: right_map[i], other, store_right)
            else:
                right_map[...] = recv[0]
                left_map[0] = eye
                left_map[1] = zero

        @pl.when(bit_of(r) == 1)
        def _():
            if r > 0:
                arrive(0, 0)
                settle(0, 0)
                needs = (None, functools.partial(arrive, 0, 1), functools.partial(settle, 0, 1))
            else:
                needs = (None, None, None)
            joined(other, mine, store_total, needs)
            if r > 0:
                new = product(left_map[0], pair(other(0), other(1)))
                left_map[0] = new[:, :w]
                left_map[1] = new[:, w:] + left_map[1]
            else:
                left_map[...] = recv[0, 0:2]
                right_map[0] = eye
                right_map[1] = zero
                right_map[2] = zero
                right_map[3] = zero

    r = rounds - 1
    stack = maps[...].reshape(2 * w, w)
    tail = pair(tails[0], tails[1])

    def finish(y):
        rest = y[w:] - product(right_map[2], y[w:]) - right_map[3]
        x = product(tail, rest, True)
        return x[:w], x[w:] + product(inverses[0, 0], y[:w], True)

    def put(x1, x0):
        white[...] = jnp.concatenate([x0, x1], 0).reshape(tx, ty, count)

    @pl.when(bit_of(r) == 0)
    def _():
        x1, x0 = finish(values[...].reshape(2 * w, count) + product(stack, left_map[1]))
        back = product(right_map[0], tail)
        receive(r, 1)
        middle = product(recv[r, 2], total[r, 1]) + recv[r, 3]
        change = product(back, middle, True)
        put(x1 - change[:w], x0 - change[w:])

    @pl.when(bit_of(r) == 1)
    def _():
        new = product(stack, pair(left_map[0], left_map[1]))
        base = values[...].reshape(2 * w, count) + new[:, w:]
        receive(r, 0)
        put(*finish(base + product(new[:, :w], recv[r, 1])))

    out = white[...]
    grad[0] = jnp.sum(out * samples[...], axis=2) * (1.0 / count)
    grad[1] = jnp.sum(out * lap_x[...], axis=2) * (1.0 / count)
    grad[2] = jnp.sum(out * lap_y[...], axis=2) * (1.0 / count)

    for i in range(4):
        @pl.when(neighbours[i][0])
        def _(i=i):
            halos[i].wait_send()
    swap(0).wait_send()
    swap(1).wait_send()
    for r in range(1, rounds - 1):
        for side in range(2):
            @pl.when(bit_of(r) == side)
            def _(r=r, side=side):
                for k in range(2):
                    give(r, side, k).wait_send()
                    hand(r, 1 - side, k).wait_send()
    for part in range(2):
        @pl.when(bit_of(rounds - 1) == part)
        def _(part=part):
            direct(rounds - 1, part, core).wait_send()
            relay(rounds - 1, 1 - part, core).wait_send()


def body(n_front, n_lat, *arrays):
    samples, inverses = arrays[0], arrays[4]
    tx, ty, count = samples.shape
    w = inverses.shape[-1]
    rounds = n_lat.bit_length() + n_front.bit_length() - 2
    vmem = pl.BlockSpec(memory_space=pltpu.VMEM)
    return pl.pallas_call(
        functools.partial(kernel, n_front, n_lat),
        out_shape=(pltpu.VMEM((tx, ty, count), F32), pltpu.VMEM((3, tx, ty), F32)),
        in_specs=[pl.BlockSpec(memory_space=pltpu.HBM)] * 6,
        out_specs=(vmem, vmem),
        scratch_shapes=[
            *[pltpu.VMEM(a.shape, F32) for a in arrays],
            pltpu.SemaphoreType.DMA((6,)),
            pltpu.VMEM((tx, ty, count), F32),
            pltpu.VMEM((tx, ty, count), F32),
            pltpu.VMEM((2, tx, count), F32),
            pltpu.VMEM((2, ty, count), F32),
            pltpu.VMEM((2, tx, count), F32),
            pltpu.VMEM((2, w, w), F32),
            pltpu.VMEM((2, w, w), F32),
            pltpu.VMEM((2, w, count), F32),
            pltpu.VMEM((4, w, w), F32),
            pltpu.VMEM((2, w, w), F32),
            pltpu.VMEM((rounds, 4, w, w), F32),
            pltpu.VMEM((rounds, 4, w, w), F32),
            pltpu.SemaphoreType.DMA((4,)),
            pltpu.SemaphoreType.DMA((4,)),
            pltpu.SemaphoreType.DMA((rounds, 4)),
            pltpu.SemaphoreType.DMA((rounds, 4)),
        ],
        compiler_params=pltpu.CompilerParams(
            collective_id=0, has_side_effects=True, vmem_limit_bytes=48 * 1024 * 1024),
    )(*[pltpu.with_memory_space_constraint(a, pltpu.HBM) for a in arrays])


def solution(mesh):
    placed = (
        P("front", "lat", None),
        P("front", "lat"),
        P("front", "lat"),
        P("front", "lat"),
        P("front", "lat", None, None),
        P("front", "lat", None, None),
    )
    return jax.shard_map(
        functools.partial(body, mesh.shape["front"], mesh.shape["lat"]),
        mesh=mesh,
        in_specs=placed,
        out_specs=(P("front", "lat", None), P(None, "front", "lat")),
        check_vma=False,
    )
```

```python
import functools
import jax
import jax.numpy as jnp
from jax import lax
from jax.experimental import pallas as pl
from jax.experimental.pallas import tpu as pltpu
from jax.sharding import PartitionSpec as P

MESH = pl.DeviceIdType.MESH
F32 = jnp.float32
BF16 = jnp.bfloat16


def split(value):
    high = value.astype(BF16)
    return high, (value - high.astype(F32)).astype(BF16)


def product(left, right, transposed=False):
    dim = 0 if transposed else 1
    lh, ll = split(left)
    rh, rl = split(right)
    return lax.dot_general(
        jnp.concatenate([lh, ll, lh], axis=dim),
        jnp.concatenate([rh, rh, rl], axis=0),
        (((dim,), (0,)), ((), ())),
        preferred_element_type=F32,
    )


def pair(left, right):
    return jnp.concatenate([left, right], axis=1)


def kernel(n_front, n_lat, samples_in, reaction_in, weight_x_in, weight_y_in, inverses_in, couplings_in,
           white, grad, samples, reaction, weight_x, weight_y, inverses, couplings, loads, lap_x, lap_y, edges, halo_x, halo_y, maps, tails, values, right_map, left_map,
           total, recv, halo_send, halo_recv, sends, recvs):
    front, lat = lax.axis_index("front"), lax.axis_index("lat")
    lat_rounds = n_lat.bit_length() - 1
    rounds = lat_rounds + n_front.bit_length() - 1
    tx, ty, count = samples.shape
    w = inverses.shape[-1]

    def bit_of(r):
        if r < lat_rounds:
            return lax.rem(lax.div(lat, 1 << r), 2)
        return lax.rem(lax.div(front, 1 << (r - lat_rounds)), 2)

    def partner(r):
        sign = 1 - 2 * bit_of(r)
        if r < lat_rounds:
            return (front, lat + sign * (1 << r))
        return (front + sign * (1 << (r - lat_rounds)), lat)

    neighbours = (
        (front < n_front - 1, (front + 1, lat)),
        (front > 0, (front - 1, lat)),
        (lat < n_lat - 1, (front, lat + 1)),
        (lat > 0, (front, lat - 1)),
    )

    inputs = [
        pltpu.make_async_copy(source, here, loads.at[i]) for i, (source, here) in enumerate((
            (samples_in, samples), (reaction_in, reaction), (weight_x_in, weight_x),
            (weight_y_in, weight_y), (inverses_in, inverses), (couplings_in, couplings)))]
    for i in (0, 4, 5, 1, 2, 3):
        inputs[i].start()
    middle_step = 1 - 2 * bit_of(rounds - 1)
    neighbours_all = neighbours + (
        (bit_of(rounds - 2) != bit_of(rounds - 1),
         (front + middle_step * (1 << (rounds - 2 - lat_rounds)), lat)),)
    barrier = pltpu.get_barrier_semaphore()
    for r in range(rounds):
        pl.semaphore_signal(barrier, inc=1, device_id=partner(r), device_id_type=MESH)
    for exists, target in neighbours_all:
        @pl.when(exists)
        def _(target=target):
            pl.semaphore_signal(barrier, inc=1, device_id=target, device_id_type=MESH)

    samples_copy, reaction_copy, weight_x_copy, weight_y_copy, inverses_copy, couplings_copy = inputs
    samples_copy.wait()
    s = samples[...]
    edges[0] = s[:, ty - 1, :]
    edges[1] = s[:, 0, :]
    inverses_copy.wait()
    couplings_copy.wait()
    inv0, inv1 = inverses[0, 0], inverses[0, 1]
    t0 = -product(inv0, couplings[0, 0])
    t1 = -product(inv1, couplings[0, 1])
    maps[0] = t0

    peers = rounds
    for exists, _ in neighbours_all:
        peers = peers + exists.astype(jnp.int32)
    pl.semaphore_wait(barrier, peers)

    halos = []
    for i, (source, landing) in enumerate((
        (samples.at[tx - 1], halo_x.at[0]),
        (samples.at[0], halo_x.at[1]),
        (edges.at[0], halo_y.at[0]),
        (edges.at[1], halo_y.at[1]),
    )):
        halos.append(pltpu.make_async_remote_copy(
            src_ref=source, dst_ref=landing, send_sem=halo_send.at[i], recv_sem=halo_recv.at[i],
            device_id=neighbours[i][1], device_id_type=MESH))

        @pl.when(neighbours[i][0])
        def _(i=i):
            halos[i].start()

    full = product(t1, t0)
    maps[1] = full
    stack = maps[0:2].reshape(2 * w, w)
    total[0, 0] = full
    tail = product(t1, inv0)
    tails[0] = inv1
    tails[1] = tail
    total[0, 2] = -product(stack, stack, True)
    for i, landing in enumerate((halo_x.at[0], halo_x.at[1], halo_y.at[0], halo_y.at[1])):
        comes = neighbours[i ^ 1][0]

        @pl.when(comes)
        def _(i=i):
            halos[i].wait_recv()

        @pl.when(jnp.logical_not(comes))
        def _(landing=landing):
            landing[...] = jnp.zeros((landing.shape[0], count), F32)

    reaction_copy.wait()
    weight_x_copy.wait()
    weight_y_copy.wait()
    hx, hy = halo_x[...], halo_y[...]
    lx = 2.0 * s - jnp.concatenate([hx[0:1], s[:-1]], 0) - jnp.concatenate([s[1:], hx[1:2]], 0)
    ly = 2.0 * s - jnp.concatenate([hy[0][:, None, :], s[:, :-1]], 1) - jnp.concatenate([s[:, 1:], hy[1][:, None, :]], 1)
    lap_x[...] = lx
    lap_y[...] = ly
    resid = (reaction[...][:, :, None] * s + weight_x[...][:, :, None] * lx
             + weight_y[...][:, :, None] * ly).reshape(2 * w, count)
    y0 = product(inv0, resid[:w])
    y1 = product(pair(tail, inv1), resid)
    values[0] = y0
    values[1] = y1
    total[0, 1] = y1
    core = bit_of(0)

    def swap(part):
        window = pl.ds(2 * part, 2)
        return pltpu.make_async_remote_copy(
            src_ref=total.at[0, window], dst_ref=recv.at[0, window],
            send_sem=sends.at[0, part], recv_sem=recvs.at[0, part],
            device_id=partner(0), device_id_type=MESH)

    def piece(ref, r, kind, which):
        if kind == 0:
            return ref.at[r, 1, pl.ds(which * (w // 2), w // 2)]
        if kind == 1:
            return ref.at[r, pl.ds(2 + which, 1)]
        return ref.at[r, pl.ds(2 * which, 2)]

    def remote(source, landing, sent, arrived, target):
        return pltpu.make_async_remote_copy(
            src_ref=source, dst_ref=landing, send_sem=sent, recv_sem=arrived,
            device_id=target, device_id_type=MESH)

    def direct(r, kind, which):
        return remote(piece(total, r, kind, which), piece(recv, r, kind, which),
                      sends.at[r, 0], recvs.at[r, which], partner(r))

    def relay(r, kind, which):
        return remote(piece(recv, r, kind, which), piece(recv, r, kind, which),
                      sends.at[r, 2], recvs.at[r, which], partner(0))

    def receive(r, kind):
        direct(r, kind, core).wait_recv()
        relay(r, kind, core).start()
        relay(r, kind, 1 - core).wait_recv()

    def matrix(side, which, k):
        return which + 2 * k if side == 0 else 2 * which + k

    def give(r, side, k, which=core):
        m = matrix(side, which, k)
        return remote(total.at[r, m], recv.at[r, m], sends.at[r, k], recvs.at[r, m], partner(r))

    def hand(r, side, k, which=core):
        m = matrix(side, which, k)
        return remote(recv.at[r, m], recv.at[r, m], sends.at[r, 2 + k], recvs.at[r, m], partner(0))

    first_bit, last_bit = bit_of(rounds - 2), bit_of(rounds - 1)

    def quarter(p):
        return (first_bit == p % 2) & (last_bit == p // 2)

    def near(kind):
        r = rounds - 1
        step = (1 - 2 * kind) * (1 << (rounds - 2 - lat_rounds))
        return remote(piece(total, r, kind, core), piece(recv, r, kind, core),
                      sends.at[r, 1], recvs.at[r, core], (front + step, lat))

    def send(r, part):
        if r == rounds - 2:
            if part == 0:
                @pl.when(quarter(0))
                def _():
                    direct(r, 0, core).start()

                @pl.when(quarter(2))
                def _():
                    give(r, 0, 0).start()
            else:
                @pl.when(quarter(3))
                def _():
                    direct(r, 1, core).start()

            @pl.when(quarter(1) & (core == part))
            def _():
                give(r, 1, 0, part).start()
                give(r, 1, 1, part).start()
        else:
            @pl.when(bit_of(r) == 0)
            def _():
                give(r, 0, part).start()

            @pl.when((bit_of(r) == 1) & (core == part))
            def _():
                give(r, 1, 0, part).start()
                give(r, 1, 1, part).start()

    swap(0).start()
    total[0, 3] = -product(stack, jnp.concatenate([y0, y1], 0), True)
    swap(1).start()
    eye = (lax.broadcasted_iota(jnp.int32, (w, w), 0) == lax.broadcasted_iota(jnp.int32, (w, w), 1)).astype(F32)
    zero = jnp.zeros((w, w), F32)
    def joined(earlier, later, store, needs=(None, None, None)):
        wait = lambda i: needs[i]() if needs[i] else None
        start = earlier(0)
        ab = pair(start, earlier(1))
        both = product(jnp.concatenate([later(0), later(2)], 0), ab)
        wait(0)
        store(0, both[:w, :w], both[:w, w:] + later(1))
        wait(1)
        mid = pair(both[w:, :w], both[w:, w:] + later(3))
        new = product(start, mid, True)
        wait(2)
        store(1, earlier(2) + new[:, :w], earlier(3) + new[:, w:])

    def store_right(part, first, second):
        right_map[2 * part] = first
        right_map[2 * part + 1] = second

    for r in range(rounds - 2):
        def store_total(part, first, second, r=r):
            total[r + 1, 2 * part] = first
            total[r + 1, 2 * part + 1] = second
            send(r + 1, part)

        mine = lambda i, r=r: total[r, i]
        other = lambda i, r=r: recv[r, i]

        def arrive(side, k, r=r):
            give(r, side, k).wait_recv()
            hand(r, side, k).start()

        def settle(side, k, r=r):
            hand(r, side, k, 1 - core).wait_recv()

        if r == 0:
            swap(0).wait_recv()
            swap(1).wait_recv()

        @pl.when(bit_of(r) == 0)
        def _():
            def rest():
                arrive(1, 1)
                settle(1, 1)

            if r > 0:
                arrive(1, 0)
                settle(1, 0)
            joined(mine, other, store_total, (rest if r > 0 else None, None, None))
            if r > 0:
                joined(lambda i: right_map[i], other, store_right)
            else:
                right_map[...] = recv[0]
                left_map[0] = eye
                left_map[1] = zero

        @pl.when(bit_of(r) == 1)
        def _():
            if r > 0:
                arrive(0, 0)
                settle(0, 0)
                needs = (None, functools.partial(arrive, 0, 1), functools.partial(settle, 0, 1))
            else:
                needs = (None, None, None)
            joined(other, mine, store_total, needs)
            if r > 0:
                new = product(left_map[0], pair(other(0), other(1)))
                left_map[0] = new[:, :w]
                left_map[1] = new[:, w:] + left_map[1]
            else:
                left_map[...] = recv[0, 0:2]
                right_map[0] = eye
                right_map[1] = zero
                right_map[2] = zero
                right_map[3] = zero

    r = rounds - 2

    def quarter_arrive(side, k):
        give(r, side, k).wait_recv()
        hand(r, side, k).start()
        hand(r, side, k, 1 - core).wait_recv()

    @pl.when(quarter(0))
    def _():
        quarter_arrive(1, 0)
        quarter_arrive(1, 1)
        total[r + 1, 1] = product(recv[r, 0], total[r, 1]) + recv[r, 1]
        joined(lambda i: right_map[i], lambda i: recv[r, i], store_right)

    @pl.when(quarter(1))
    def _():
        receive(r, 0)
        total[r + 1, 1] = product(total[r, 0], recv[r, 1]) + total[r, 1]
        direct(r + 1, 0, core).start()
        near(0).start()
        left_map[1] = product(left_map[0], recv[r, 1]) + left_map[1]

    def adjoint(a, b):
        mid = product(recv[r, 2], pair(a, b))
        return product(a, pair(mid[:, :w], mid[:, w:] + recv[r, 3]), True)

    @pl.when(quarter(2))
    def _():
        receive(r, 1)
        new = adjoint(total[r, 0], total[r, 1])
        total[r + 1, 2] = total[r, 2] + new[:, :w]
        total[r + 1, 3] = total[r, 3] + new[:, w:]
        direct(r + 1, 1, core).start()
        near(1).start()
        new = adjoint(right_map[0], right_map[1])
        right_map[2] = right_map[2] + new[:, :w]
        right_map[3] = right_map[3] + new[:, w:]

    @pl.when(quarter(3))
    def _():
        quarter_arrive(0, 0)
        new = product(left_map[0], pair(recv[r, 0], recv[r, 1]))
        left_map[0] = new[:, :w]
        left_map[1] = new[:, w:] + left_map[1]

    z = rounds - 1
    stack = maps[...].reshape(2 * w, w)
    tail = pair(tails[0], tails[1])

    def finish(y):
        rest = y[w:] - product(right_map[2], y[w:]) - right_map[3]
        x = product(tail, rest, True)
        return x[:w], x[w:] + product(inverses[0, 0], y[:w], True)

    def put(x1, x0):
        white[...] = jnp.concatenate([x0, x1], 0).reshape(tx, ty, count)

    @pl.when(last_bit == 0)
    def _():
        x1, x0 = finish(values[...].reshape(2 * w, count) + product(stack, left_map[1]))
        back = product(right_map[0], tail)
        receive(z, 1)
        middle = product(recv[z, 2], total[z, 1]) + recv[z, 3]
        change = product(back, middle, True)
        put(x1 - change[:w], x0 - change[w:])

    @pl.when(last_bit == 1)
    def _():
        new = product(stack, pair(left_map[0], left_map[1]))
        base = values[...].reshape(2 * w, count) + new[:, w:]
        receive(z, 0)
        put(*finish(base + product(new[:, :w], recv[z, 1])))

    out = white[...]
    grad[0] = jnp.sum(out * samples[...], axis=2) * (1.0 / count)
    grad[1] = jnp.sum(out * lap_x[...], axis=2) * (1.0 / count)
    grad[2] = jnp.sum(out * lap_y[...], axis=2) * (1.0 / count)

    for i in range(4):
        @pl.when(neighbours[i][0])
        def _(i=i):
            halos[i].wait_send()
    swap(0).wait_send()
    swap(1).wait_send()
    for r in range(1, rounds - 2):
        for side in range(2):
            @pl.when(bit_of(r) == side)
            def _(r=r, side=side):
                for k in range(2):
                    give(r, side, k).wait_send()
                    hand(r, 1 - side, k).wait_send()
    r, z = rounds - 2, rounds - 1
    for p, started in enumerate((
        (direct(r, 0, core), hand(r, 1, 0), hand(r, 1, 1)),
        (give(r, 1, 0), give(r, 1, 1), relay(r, 0, core), direct(z, 0, core), near(0)),
        (give(r, 0, 0), relay(r, 1, core), direct(z, 1, core), near(1)),
        (direct(r, 1, core), hand(r, 0, 0)),
    )):
        @pl.when(quarter(p))
        def _(p=p, started=started):
            for one in started + (relay(z, 1 - p // 2, core),):
                one.wait_send()


def body(n_front, n_lat, *arrays):
    samples, inverses = arrays[0], arrays[4]
    tx, ty, count = samples.shape
    w = inverses.shape[-1]
    rounds = n_lat.bit_length() + n_front.bit_length() - 2
    vmem = pl.BlockSpec(memory_space=pltpu.VMEM)
    return pl.pallas_call(
        functools.partial(kernel, n_front, n_lat),
        out_shape=(pltpu.VMEM((tx, ty, count), F32), pltpu.VMEM((3, tx, ty), F32)),
        in_specs=[pl.BlockSpec(memory_space=pltpu.HBM)] * 6,
        out_specs=(vmem, vmem),
        scratch_shapes=[
            *[pltpu.VMEM(a.shape, F32) for a in arrays],
            pltpu.SemaphoreType.DMA((6,)),
            pltpu.VMEM((tx, ty, count), F32),
            pltpu.VMEM((tx, ty, count), F32),
            pltpu.VMEM((2, tx, count), F32),
            pltpu.VMEM((2, ty, count), F32),
            pltpu.VMEM((2, tx, count), F32),
            pltpu.VMEM((2, w, w), F32),
            pltpu.VMEM((2, w, w), F32),
            pltpu.VMEM((2, w, count), F32),
            pltpu.VMEM((4, w, w), F32),
            pltpu.VMEM((2, w, w), F32),
            pltpu.VMEM((rounds, 4, w, w), F32),
            pltpu.VMEM((rounds, 4, w, w), F32),
            pltpu.SemaphoreType.DMA((4,)),
            pltpu.SemaphoreType.DMA((4,)),
            pltpu.SemaphoreType.DMA((rounds, 4)),
            pltpu.SemaphoreType.DMA((rounds, 4)),
        ],
        compiler_params=pltpu.CompilerParams(
            collective_id=0, has_side_effects=True, vmem_limit_bytes=48 * 1024 * 1024),
    )(*[pltpu.with_memory_space_constraint(a, pltpu.HBM) for a in arrays])


def solution(mesh):
    placed = (
        P("front", "lat", None),
        P("front", "lat"),
        P("front", "lat"),
        P("front", "lat"),
        P("front", "lat", None, None),
        P("front", "lat", None, None),
    )
    return jax.shard_map(
        functools.partial(body, mesh.shape["front"], mesh.shape["lat"]),
        mesh=mesh,
        in_specs=placed,
        out_specs=(P("front", "lat", None), P(None, "front", "lat")),
        check_vma=False,
    )
```

```python
import functools
import jax
import jax.numpy as jnp
from jax import lax
from jax.experimental import pallas as pl
from jax.experimental.pallas import tpu as pltpu
from jax.sharding import PartitionSpec as P

MESH = pl.DeviceIdType.MESH
F32 = jnp.float32
BF16 = jnp.bfloat16


def split(value):
    high = value.astype(BF16)
    return high, (value - high.astype(F32)).astype(BF16)


def product(left, right, transposed=False):
    dim = 0 if transposed else 1
    lh, ll = split(left)
    rh, rl = split(right)
    return lax.dot_general(
        jnp.concatenate([lh, ll, lh], axis=dim),
        jnp.concatenate([rh, rh, rl], axis=0),
        (((dim,), (0,)), ((), ())),
        preferred_element_type=F32,
    )


def pair(left, right):
    return jnp.concatenate([left, right], axis=1)


def kernel(n_front, n_lat, samples_in, reaction_in, weight_x_in, weight_y_in, inverses_in, couplings_in,
           white, grad, samples, reaction, weight_x, weight_y, inverses, couplings, loads, lap_x, lap_y, edges, halo_x, halo_y, maps, tails, values, right_map, left_map,
           total, recv, halo_send, halo_recv, sends, recvs):
    front, lat = lax.axis_index("front"), lax.axis_index("lat")
    lat_rounds = n_lat.bit_length() - 1
    rounds = lat_rounds + n_front.bit_length() - 1
    tx, ty, count = samples.shape
    w = inverses.shape[-1]

    def bit_of(r):
        if r < lat_rounds:
            return lax.rem(lax.div(lat, 1 << r), 2)
        return lax.rem(lax.div(front, 1 << (r - lat_rounds)), 2)

    def partner(r):
        sign = 1 - 2 * bit_of(r)
        if r < lat_rounds:
            return (front, lat + sign * (1 << r))
        return (front + sign * (1 << (r - lat_rounds)), lat)

    neighbours = (
        (front < n_front - 1, (front + 1, lat)),
        (front > 0, (front - 1, lat)),
        (lat < n_lat - 1, (front, lat + 1)),
        (lat > 0, (front, lat - 1)),
    )

    inputs = [
        pltpu.make_async_copy(source, here, loads.at[i]) for i, (source, here) in enumerate((
            (samples_in, samples), (reaction_in, reaction), (weight_x_in, weight_x),
            (weight_y_in, weight_y), (inverses_in, inverses), (couplings_in, couplings)))]
    for i in (0, 4, 5, 1, 2, 3):
        inputs[i].start()
    middle_step = 1 - 2 * bit_of(rounds - 1)
    neighbours_all = neighbours + (
        (bit_of(rounds - 2) != bit_of(rounds - 1),
         (front + middle_step * (1 << (rounds - 2 - lat_rounds)), lat)),)
    barrier = pltpu.get_barrier_semaphore()
    for r in range(rounds):
        pl.semaphore_signal(barrier, inc=1, device_id=partner(r), device_id_type=MESH)
    for exists, target in neighbours_all:
        @pl.when(exists)
        def _(target=target):
            pl.semaphore_signal(barrier, inc=1, device_id=target, device_id_type=MESH)

    samples_copy, reaction_copy, weight_x_copy, weight_y_copy, inverses_copy, couplings_copy = inputs
    samples_copy.wait()
    s = samples[...]
    edges[0] = s[:, ty - 1, :]
    edges[1] = s[:, 0, :]
    inverses_copy.wait()
    couplings_copy.wait()
    inv0, inv1 = inverses[0, 0], inverses[0, 1]
    t0 = -product(inv0, couplings[0, 0])
    t1 = -product(inv1, couplings[0, 1])
    maps[0] = t0

    peers = rounds
    for exists, _ in neighbours_all:
        peers = peers + exists.astype(jnp.int32)
    pl.semaphore_wait(barrier, peers)

    halos = []
    for i, (source, landing) in enumerate((
        (samples.at[tx - 1], halo_x.at[0]),
        (samples.at[0], halo_x.at[1]),
        (edges.at[0], halo_y.at[0]),
        (edges.at[1], halo_y.at[1]),
    )):
        halos.append(pltpu.make_async_remote_copy(
            src_ref=source, dst_ref=landing, send_sem=halo_send.at[i], recv_sem=halo_recv.at[i],
            device_id=neighbours[i][1], device_id_type=MESH))

        @pl.when(neighbours[i][0])
        def _(i=i):
            halos[i].start()

    core = bit_of(0)

    def swap(m):
        return pltpu.make_async_remote_copy(
            src_ref=total.at[0, m], dst_ref=recv.at[0, m],
            send_sem=sends.at[0, m], recv_sem=recvs.at[0, m],
            device_id=partner(0), device_id_type=MESH)

    def piece(ref, r, kind, which):
        if kind == 0:
            return ref.at[r, 1, pl.ds(which * (w // 2), w // 2)]
        if kind == 1:
            return ref.at[r, pl.ds(2 + which, 1)]
        return ref.at[r, pl.ds(2 * which, 2)]

    def remote(source, landing, sent, arrived, target):
        return pltpu.make_async_remote_copy(
            src_ref=source, dst_ref=landing, send_sem=sent, recv_sem=arrived,
            device_id=target, device_id_type=MESH)

    def direct(r, kind, which):
        return remote(piece(total, r, kind, which), piece(recv, r, kind, which),
                      sends.at[r, 0], recvs.at[r, which], partner(r))

    def relay(r, kind, which):
        return remote(piece(recv, r, kind, which), piece(recv, r, kind, which),
                      sends.at[r, 2], recvs.at[r, which], partner(0))

    def receive(r, kind):
        direct(r, kind, core).wait_recv()
        relay(r, kind, core).start()
        relay(r, kind, 1 - core).wait_recv()

    def matrix(side, which, k):
        return which + 2 * k if side == 0 else 2 * which + k

    def give(r, side, k, which=core):
        m = matrix(side, which, k)
        return remote(total.at[r, m], recv.at[r, m], sends.at[r, k], recvs.at[r, m], partner(r))

    def hand(r, side, k, which=core):
        m = matrix(side, which, k)
        return remote(recv.at[r, m], recv.at[r, m], sends.at[r, 2 + k], recvs.at[r, m], partner(0))

    first_bit, last_bit = bit_of(rounds - 2), bit_of(rounds - 1)

    def quarter(p):
        return (first_bit == p % 2) & (last_bit == p // 2)

    def near(kind):
        r = rounds - 1
        step = (1 - 2 * kind) * (1 << (rounds - 2 - lat_rounds))
        return remote(piece(total, r, kind, core), piece(recv, r, kind, core),
                      sends.at[r, 1], recvs.at[r, core], (front + step, lat))

    def send(r, part):
        if r == rounds - 2:
            if part == 0:
                @pl.when(quarter(0))
                def _():
                    direct(r, 0, core).start()

                @pl.when(quarter(2))
                def _():
                    give(r, 0, 0).start()
            else:
                @pl.when(quarter(3))
                def _():
                    direct(r, 1, core).start()

            @pl.when(quarter(1) & (core == part))
            def _():
                give(r, 1, 0, part).start()
                give(r, 1, 1, part).start()
        else:
            @pl.when(bit_of(r) == 0)
            def _():
                give(r, 0, part).start()

            @pl.when((bit_of(r) == 1) & (core == part))
            def _():
                give(r, 1, 0, part).start()
                give(r, 1, 1, part).start()

    full = product(t1, t0)
    maps[1] = full
    total[0, 0] = full
    swap(0).start()
    stack = maps[0:2].reshape(2 * w, w)
    total[0, 2] = -product(stack, stack, True)
    swap(2).start()
    tail = product(t1, inv0)
    tails[0] = inv1
    tails[1] = tail

    def first_matrices(earlier, later):
        start = earlier[0, 0]
        both = product(jnp.concatenate([later[0, 0], later[0, 2]], 0), start)
        total[1, 0] = both[:w]
        total[1, 2] = earlier[0, 2] + product(start, both[w:], True)

    def first_vectors(earlier, later):
        both = product(jnp.concatenate([later[0, 0], later[0, 2]], 0), earlier[0, 1])
        total[1, 1] = both[:w] + later[0, 1]

        @pl.when(core == 0)
        def _():
            give(1, 1, 1, 0).start()

        total[1, 3] = earlier[0, 3] + product(earlier[0, 0], both[w:] + later[0, 3], True)

        @pl.when(core == 1)
        def _():
            give(1, 1, 1, 1).start()

    def first(step):
        @pl.when(core == 0)
        def _():
            step(total, recv)

        @pl.when(core == 1)
        def _():
            step(recv, total)

    swap(0).wait_recv()
    swap(2).wait_recv()
    first(first_matrices)
    give(1, 1, 0).start()
    for i, landing in enumerate((halo_x.at[0], halo_x.at[1], halo_y.at[0], halo_y.at[1])):
        comes = neighbours[i ^ 1][0]

        @pl.when(comes)
        def _(i=i):
            halos[i].wait_recv()

        @pl.when(jnp.logical_not(comes))
        def _(landing=landing):
            landing[...] = jnp.zeros((landing.shape[0], count), F32)

    reaction_copy.wait()
    weight_x_copy.wait()
    weight_y_copy.wait()
    hx, hy = halo_x[...], halo_y[...]
    lx = 2.0 * s - jnp.concatenate([hx[0:1], s[:-1]], 0) - jnp.concatenate([s[1:], hx[1:2]], 0)
    ly = 2.0 * s - jnp.concatenate([hy[0][:, None, :], s[:, :-1]], 1) - jnp.concatenate([s[:, 1:], hy[1][:, None, :]], 1)
    lap_x[...] = lx
    lap_y[...] = ly
    resid = (reaction[...][:, :, None] * s + weight_x[...][:, :, None] * lx
             + weight_y[...][:, :, None] * ly).reshape(2 * w, count)
    y0 = product(inv0, resid[:w])
    y1 = product(pair(tail, inv1), resid)
    values[0] = y0
    values[1] = y1
    total[0, 1] = y1
    swap(1).start()
    total[0, 3] = -product(stack, jnp.concatenate([y0, y1], 0), True)
    swap(3).start()
    swap(1).wait_recv()
    swap(3).wait_recv()
    first(first_vectors)
    eye = (lax.broadcasted_iota(jnp.int32, (w, w), 0) == lax.broadcasted_iota(jnp.int32, (w, w), 1)).astype(F32)
    zero = jnp.zeros((w, w), F32)

    @pl.when(core == 0)
    def _():
        right_map[...] = recv[0]
        left_map[0] = eye
        left_map[1] = zero

    @pl.when(core == 1)
    def _():
        left_map[...] = recv[0, 0:2]
        right_map[0] = eye
        right_map[1] = zero
        right_map[2] = zero
        right_map[3] = zero

    def joined(earlier, later, store, needs=(None, None, None)):
        wait = lambda i: needs[i]() if needs[i] else None
        start = earlier(0)
        ab = pair(start, earlier(1))
        both = product(jnp.concatenate([later(0), later(2)], 0), ab)
        wait(0)
        store(0, both[:w, :w], both[:w, w:] + later(1))
        wait(1)
        mid = pair(both[w:, :w], both[w:, w:] + later(3))
        new = product(start, mid, True)
        wait(2)
        store(1, earlier(2) + new[:, :w], earlier(3) + new[:, w:])

    def store_right(part, first, second):
        right_map[2 * part] = first
        right_map[2 * part + 1] = second

    for r in range(1, rounds - 2):
        def store_total(part, first, second, r=r):
            total[r + 1, 2 * part] = first
            total[r + 1, 2 * part + 1] = second
            send(r + 1, part)

        mine = lambda i, r=r: total[r, i]
        other = lambda i, r=r: recv[r, i]

        def arrive(side, k, r=r):
            give(r, side, k).wait_recv()
            hand(r, side, k).start()

        def settle(side, k, r=r):
            hand(r, side, k, 1 - core).wait_recv()

        @pl.when(bit_of(r) == 0)
        def _():
            def rest():
                arrive(1, 1)
                settle(1, 1)

            arrive(1, 0)
            settle(1, 0)
            joined(mine, other, store_total, (rest, None, None))
            joined(lambda i: right_map[i], other, store_right)

        @pl.when(bit_of(r) == 1)
        def _():
            if r == 1:
                for k in range(2):
                    arrive(1, k)
                    settle(1, k)
                joined(other, mine, store_total)
            else:
                arrive(0, 0)
                settle(0, 0)
                joined(other, mine, store_total, (
                    None, functools.partial(arrive, 0, 1), functools.partial(settle, 0, 1)))
            new = product(left_map[0], pair(other(0), other(1)))
            left_map[0] = new[:, :w]
            left_map[1] = new[:, w:] + left_map[1]

    r = rounds - 2

    def quarter_arrive(side, k):
        give(r, side, k).wait_recv()
        hand(r, side, k).start()
        hand(r, side, k, 1 - core).wait_recv()

    @pl.when(quarter(0))
    def _():
        quarter_arrive(1, 0)
        quarter_arrive(1, 1)
        total[r + 1, 1] = product(recv[r, 0], total[r, 1]) + recv[r, 1]
        joined(lambda i: right_map[i], lambda i: recv[r, i], store_right)

    @pl.when(quarter(1))
    def _():
        receive(r, 0)
        total[r + 1, 1] = product(total[r, 0], recv[r, 1]) + total[r, 1]
        direct(r + 1, 0, core).start()
        near(0).start()
        left_map[1] = product(left_map[0], recv[r, 1]) + left_map[1]

    def adjoint(a, b):
        mid = product(recv[r, 2], pair(a, b))
        return product(a, pair(mid[:, :w], mid[:, w:] + recv[r, 3]), True)

    @pl.when(quarter(2))
    def _():
        receive(r, 1)
        new = adjoint(total[r, 0], total[r, 1])
        total[r + 1, 2] = total[r, 2] + new[:, :w]
        total[r + 1, 3] = total[r, 3] + new[:, w:]
        direct(r + 1, 1, core).start()
        near(1).start()
        new = adjoint(right_map[0], right_map[1])
        right_map[2] = right_map[2] + new[:, :w]
        right_map[3] = right_map[3] + new[:, w:]

    @pl.when(quarter(3))
    def _():
        quarter_arrive(0, 0)
        new = product(left_map[0], pair(recv[r, 0], recv[r, 1]))
        left_map[0] = new[:, :w]
        left_map[1] = new[:, w:] + left_map[1]

    z = rounds - 1
    stack = maps[...].reshape(2 * w, w)
    tail = pair(tails[0], tails[1])

    def finish(y):
        rest = y[w:] - product(right_map[2], y[w:]) - right_map[3]
        x = product(tail, rest, True)
        return x[:w], x[w:] + product(inverses[0, 0], y[:w], True)

    def put(x1, x0):
        white[...] = jnp.concatenate([x0, x1], 0).reshape(tx, ty, count)

    @pl.when(last_bit == 0)
    def _():
        x1, x0 = finish(values[...].reshape(2 * w, count) + product(stack, left_map[1]))
        back = product(right_map[0], tail)
        receive(z, 1)
        middle = product(recv[z, 2], total[z, 1]) + recv[z, 3]
        change = product(back, middle, True)
        put(x1 - change[:w], x0 - change[w:])

    @pl.when(last_bit == 1)
    def _():
        new = product(stack, pair(left_map[0], left_map[1]))
        base = values[...].reshape(2 * w, count) + new[:, w:]
        receive(z, 0)
        put(*finish(base + product(new[:, :w], recv[z, 1])))

    out = white[...]
    grad[0] = jnp.sum(out * samples[...], axis=2) * (1.0 / count)
    grad[1] = jnp.sum(out * lap_x[...], axis=2) * (1.0 / count)
    grad[2] = jnp.sum(out * lap_y[...], axis=2) * (1.0 / count)

    for i in range(4):
        @pl.when(neighbours[i][0])
        def _(i=i):
            halos[i].wait_send()
    for m in range(4):
        swap(m).wait_send()
    for k in range(2):
        give(1, 1, k).wait_send()
        hand(1, 1, k).wait_send()
    for r in range(2, rounds - 2):
        for side in range(2):
            @pl.when(bit_of(r) == side)
            def _(r=r, side=side):
                for k in range(2):
                    give(r, side, k).wait_send()
                    hand(r, 1 - side, k).wait_send()
    r, z = rounds - 2, rounds - 1
    for p, started in enumerate((
        (direct(r, 0, core), hand(r, 1, 0), hand(r, 1, 1)),
        (give(r, 1, 0), give(r, 1, 1), relay(r, 0, core), direct(z, 0, core), near(0)),
        (give(r, 0, 0), relay(r, 1, core), direct(z, 1, core), near(1)),
        (direct(r, 1, core), hand(r, 0, 0)),
    )):
        @pl.when(quarter(p))
        def _(p=p, started=started):
            for one in started + (relay(z, 1 - p // 2, core),):
                one.wait_send()


def body(n_front, n_lat, *arrays):
    samples, inverses = arrays[0], arrays[4]
    tx, ty, count = samples.shape
    w = inverses.shape[-1]
    rounds = n_lat.bit_length() + n_front.bit_length() - 2
    vmem = pl.BlockSpec(memory_space=pltpu.VMEM)
    return pl.pallas_call(
        functools.partial(kernel, n_front, n_lat),
        out_shape=(pltpu.VMEM((tx, ty, count), F32), pltpu.VMEM((3, tx, ty), F32)),
        in_specs=[pl.BlockSpec(memory_space=pltpu.HBM)] * 6,
        out_specs=(vmem, vmem),
        scratch_shapes=[
            *[pltpu.VMEM(a.shape, F32) for a in arrays],
            pltpu.SemaphoreType.DMA((6,)),
            pltpu.VMEM((tx, ty, count), F32),
            pltpu.VMEM((tx, ty, count), F32),
            pltpu.VMEM((2, tx, count), F32),
            pltpu.VMEM((2, ty, count), F32),
            pltpu.VMEM((2, tx, count), F32),
            pltpu.VMEM((2, w, w), F32),
            pltpu.VMEM((2, w, w), F32),
            pltpu.VMEM((2, w, count), F32),
            pltpu.VMEM((4, w, w), F32),
            pltpu.VMEM((2, w, w), F32),
            pltpu.VMEM((rounds, 4, w, w), F32),
            pltpu.VMEM((rounds, 4, w, w), F32),
            pltpu.SemaphoreType.DMA((4,)),
            pltpu.SemaphoreType.DMA((4,)),
            pltpu.SemaphoreType.DMA((rounds, 4)),
            pltpu.SemaphoreType.DMA((rounds, 4)),
        ],
        compiler_params=pltpu.CompilerParams(
            collective_id=0, has_side_effects=True, vmem_limit_bytes=48 * 1024 * 1024),
    )(*[pltpu.with_memory_space_constraint(a, pltpu.HBM) for a in arrays])


def solution(mesh):
    placed = (
        P("front", "lat", None),
        P("front", "lat"),
        P("front", "lat"),
        P("front", "lat"),
        P("front", "lat", None, None),
        P("front", "lat", None, None),
    )
    return jax.shard_map(
        functools.partial(body, mesh.shape["front"], mesh.shape["lat"]),
        mesh=mesh,
        in_specs=placed,
        out_specs=(P("front", "lat", None), P(None, "front", "lat")),
        check_vma=False,
    )
```

```python
import functools
import jax
import jax.numpy as jnp
from jax import lax
from jax.experimental import pallas as pl
from jax.experimental.pallas import tpu as pltpu
from jax.sharding import PartitionSpec as P

MESH = pl.DeviceIdType.MESH
F32 = jnp.float32
BF16 = jnp.bfloat16


def split(value):
    high = value.astype(BF16)
    return high, (value - high.astype(F32)).astype(BF16)


def product(left, right, transposed=False):
    dim = 0 if transposed else 1
    lh, ll = split(left)
    rh, rl = split(right)
    return lax.dot_general(
        jnp.concatenate([lh, ll, lh], axis=dim),
        jnp.concatenate([rh, rh, rl], axis=0),
        (((dim,), (0,)), ((), ())),
        preferred_element_type=F32,
    )


def pair(left, right):
    return jnp.concatenate([left, right], axis=1)


def kernel(n_front, n_lat, samples_in, reaction_in, weight_x_in, weight_y_in, inverses_in, couplings_in,
           white, grad, samples, reaction, weight_x, weight_y, inverses, couplings, loads, lap_x, lap_y, edges, halo_x, halo_y, maps, tails, values, right_map, left_map,
           total, recv, halo_send, halo_recv, sends, recvs):
    front, lat = lax.axis_index("front"), lax.axis_index("lat")
    lat_rounds = n_lat.bit_length() - 1
    rounds = lat_rounds + n_front.bit_length() - 1
    tx, ty, count = samples.shape
    w = inverses.shape[-1]

    def bit_of(r):
        if r < lat_rounds:
            return lax.rem(lax.div(lat, 1 << r), 2)
        return lax.rem(lax.div(front, 1 << (r - lat_rounds)), 2)

    def partner(r):
        sign = 1 - 2 * bit_of(r)
        if r < lat_rounds:
            return (front, lat + sign * (1 << r))
        return (front + sign * (1 << (r - lat_rounds)), lat)

    neighbours = (
        (front < n_front - 1, (front + 1, lat)),
        (front > 0, (front - 1, lat)),
        (lat < n_lat - 1, (front, lat + 1)),
        (lat > 0, (front, lat - 1)),
    )

    inputs = [
        pltpu.make_async_copy(source, here, loads.at[i]) for i, (source, here) in enumerate((
            (samples_in, samples), (reaction_in, reaction), (weight_x_in, weight_x),
            (weight_y_in, weight_y), (inverses_in, inverses), (couplings_in, couplings)))]
    for i in (0, 4, 5, 1, 2, 3):
        inputs[i].start()
    middle_step = 1 - 2 * bit_of(rounds - 1)
    neighbours_all = neighbours + (
        (bit_of(rounds - 2) != bit_of(rounds - 1),
         (front + middle_step * (1 << (rounds - 2 - lat_rounds)), lat)),)
    barrier = pltpu.get_barrier_semaphore()
    for r in range(rounds):
        pl.semaphore_signal(barrier, inc=1, device_id=partner(r), device_id_type=MESH)
    for exists, target in neighbours_all:
        @pl.when(exists)
        def _(target=target):
            pl.semaphore_signal(barrier, inc=1, device_id=target, device_id_type=MESH)

    samples_copy, reaction_copy, weight_x_copy, weight_y_copy, inverses_copy, couplings_copy = inputs
    samples_copy.wait()
    s = samples[...]
    edges[0] = s[:, ty - 1, :]
    edges[1] = s[:, 0, :]
    inverses_copy.wait()
    couplings_copy.wait()
    inv0, inv1 = inverses[0, 0], inverses[0, 1]
    t0 = -product(inv0, couplings[0, 0])
    t1 = -product(inv1, couplings[0, 1])
    maps[0] = t0

    peers = rounds
    for exists, _ in neighbours_all:
        peers = peers + exists.astype(jnp.int32)
    pl.semaphore_wait(barrier, peers)

    halos = []
    for i, (source, landing) in enumerate((
        (samples.at[tx - 1], halo_x.at[0]),
        (samples.at[0], halo_x.at[1]),
        (edges.at[0], halo_y.at[0]),
        (edges.at[1], halo_y.at[1]),
    )):
        halos.append(pltpu.make_async_remote_copy(
            src_ref=source, dst_ref=landing, send_sem=halo_send.at[i], recv_sem=halo_recv.at[i],
            device_id=neighbours[i][1], device_id_type=MESH))

        @pl.when(neighbours[i][0])
        def _(i=i):
            halos[i].start()

    core = bit_of(0)

    def swap(m):
        return pltpu.make_async_remote_copy(
            src_ref=total.at[0, m], dst_ref=recv.at[0, m],
            send_sem=sends.at[0, m], recv_sem=recvs.at[0, m],
            device_id=partner(0), device_id_type=MESH)

    def piece(ref, r, kind, which):
        if kind == 0:
            return ref.at[r, 1, pl.ds(which * (w // 2), w // 2)]
        if kind == 1:
            return ref.at[r, pl.ds(2 + which, 1)]
        return ref.at[r, pl.ds(2 * which, 2)]

    def remote(source, landing, sent, arrived, target):
        return pltpu.make_async_remote_copy(
            src_ref=source, dst_ref=landing, send_sem=sent, recv_sem=arrived,
            device_id=target, device_id_type=MESH)

    def direct(r, kind, which):
        return remote(piece(total, r, kind, which), piece(recv, r, kind, which),
                      sends.at[r, 0], recvs.at[r, which], partner(r))

    def relay(r, kind, which):
        return remote(piece(recv, r, kind, which), piece(recv, r, kind, which),
                      sends.at[r, 2], recvs.at[r, which], partner(0))

    def receive(r, kind):
        direct(r, kind, core).wait_recv()
        relay(r, kind, core).start()
        relay(r, kind, 1 - core).wait_recv()

    def matrix(side, which, k):
        return which + 2 * k if side == 0 else 2 * which + k

    def give(r, side, k, which=core):
        m = matrix(side, which, k)
        return remote(total.at[r, m], recv.at[r, m], sends.at[r, k], recvs.at[r, m], partner(r))

    def hand(r, side, k, which=core):
        m = matrix(side, which, k)
        return remote(recv.at[r, m], recv.at[r, m], sends.at[r, 2 + k], recvs.at[r, m], partner(0))

    first_bit, last_bit = bit_of(rounds - 2), bit_of(rounds - 1)

    def quarter(p):
        return (first_bit == p % 2) & (last_bit == p // 2)

    def near(kind):
        r = rounds - 1
        step = (1 - 2 * kind) * (1 << (rounds - 2 - lat_rounds))
        return remote(piece(total, r, kind, core), piece(recv, r, kind, core),
                      sends.at[r, 1], recvs.at[r, core], (front + step, lat))

    def sent(r, m):
        if r < rounds - 2:
            @pl.when(core == m // 2)
            def _():
                give(r, 1, m % 2, m // 2).start()
            return

        @pl.when(quarter(1) & (core == m // 2))
        def _():
            give(r, 1, m % 2, m // 2).start()

        if m == 1:
            @pl.when(quarter(0))
            def _():
                direct(r, 0, core).start()

        if m < 2:
            @pl.when(quarter(2) & (core == m))
            def _():
                give(r, 0, 0, m).start()
        else:
            @pl.when(quarter(3) & (core == m - 2))
            def _():
                direct(r, 1, m - 2).start()

    def matrices(r, earlier, later):
        start = earlier[r, 0]
        both = product(jnp.concatenate([later[r, 0], later[r, 2]], 0), start)
        total[r + 1, 0] = both[:w]
        sent(r + 1, 0)
        total[r + 1, 2] = earlier[r, 2] + product(start, both[w:], True)
        sent(r + 1, 2)

    def vectors(r, earlier, later):
        both = product(jnp.concatenate([later[r, 0], later[r, 2]], 0), earlier[r, 1])
        total[r + 1, 1] = both[:w] + later[r, 1]
        sent(r + 1, 1)
        total[r + 1, 3] = earlier[r, 3] + product(earlier[r, 0], both[w:] + later[r, 3], True)
        sent(r + 1, 3)

    def merge(step, r):
        @pl.when(bit_of(r) == 0)
        def _():
            step(r, total, recv)

        @pl.when(bit_of(r) == 1)
        def _():
            step(r, recv, total)

    full = product(t1, t0)
    maps[1] = full
    total[0, 0] = full
    swap(0).start()
    stack = maps[0:2].reshape(2 * w, w)
    total[0, 2] = -product(stack, stack, True)
    swap(2).start()
    tail = product(t1, inv0)
    tails[0] = inv1
    tails[1] = tail

    swap(0).wait_recv()
    swap(2).wait_recv()
    merge(matrices, 0)
    for i, landing in enumerate((halo_x.at[0], halo_x.at[1], halo_y.at[0], halo_y.at[1])):
        comes = neighbours[i ^ 1][0]

        @pl.when(comes)
        def _(i=i):
            halos[i].wait_recv()

        @pl.when(jnp.logical_not(comes))
        def _(landing=landing):
            landing[...] = jnp.zeros((landing.shape[0], count), F32)

    reaction_copy.wait()
    weight_x_copy.wait()
    weight_y_copy.wait()
    hx, hy = halo_x[...], halo_y[...]
    lx = 2.0 * s - jnp.concatenate([hx[0:1], s[:-1]], 0) - jnp.concatenate([s[1:], hx[1:2]], 0)
    ly = 2.0 * s - jnp.concatenate([hy[0][:, None, :], s[:, :-1]], 1) - jnp.concatenate([s[:, 1:], hy[1][:, None, :]], 1)
    lap_x[...] = lx
    lap_y[...] = ly
    resid = (reaction[...][:, :, None] * s + weight_x[...][:, :, None] * lx
             + weight_y[...][:, :, None] * ly).reshape(2 * w, count)
    y0 = product(inv0, resid[:w])
    y1 = product(pair(tail, inv1), resid)
    values[0] = y0
    values[1] = y1
    total[0, 1] = y1
    swap(1).start()
    total[0, 3] = -product(stack, jnp.concatenate([y0, y1], 0), True)
    swap(3).start()
    swap(1).wait_recv()
    swap(3).wait_recv()
    merge(vectors, 0)
    eye = (lax.broadcasted_iota(jnp.int32, (w, w), 0) == lax.broadcasted_iota(jnp.int32, (w, w), 1)).astype(F32)
    zero = jnp.zeros((w, w), F32)

    @pl.when(core == 0)
    def _():
        right_map[...] = recv[0]
        left_map[0] = eye
        left_map[1] = zero

    @pl.when(core == 1)
    def _():
        left_map[...] = recv[0, 0:2]
        right_map[0] = eye
        right_map[1] = zero
        right_map[2] = zero
        right_map[3] = zero

    def extend_right(other):
        start = right_map[0]
        ab = pair(start, right_map[1])
        both = product(jnp.concatenate([other[0], other[2]], 0), ab)
        right_map[0] = both[:w, :w]
        right_map[1] = both[:w, w:] + other[1]
        new = product(start, pair(both[w:, :w], both[w:, w:] + other[3]), True)
        right_map[2] = right_map[2] + new[:, :w]
        right_map[3] = right_map[3] + new[:, w:]

    def take(r, side, k):
        give(r, side, k).wait_recv()
        hand(r, side, k).start()
        hand(r, side, k, 1 - core).wait_recv()

    for r in range(1, rounds - 2):
        take(r, 1, 0)
        merge(matrices, r)
        take(r, 1, 1)
        merge(vectors, r)

        @pl.when(bit_of(r) == 0)
        def _(r=r):
            extend_right(recv.at[r])

        @pl.when(bit_of(r) == 1)
        def _(r=r):
            new = product(left_map[0], pair(recv[r, 0], recv[r, 1]))
            left_map[0] = new[:, :w]
            left_map[1] = new[:, w:] + left_map[1]

    r = rounds - 2

    @pl.when(quarter(0))
    def _():
        take(r, 1, 0)
        take(r, 1, 1)
        total[r + 1, 1] = product(recv[r, 0], total[r, 1]) + recv[r, 1]
        extend_right(recv.at[r])

    @pl.when(quarter(1))
    def _():
        receive(r, 0)
        total[r + 1, 1] = product(total[r, 0], recv[r, 1]) + total[r, 1]
        direct(r + 1, 0, core).start()
        near(0).start()
        left_map[1] = product(left_map[0], recv[r, 1]) + left_map[1]

    def adjoint(a, b):
        mid = product(recv[r, 2], pair(a, b))
        return product(a, pair(mid[:, :w], mid[:, w:] + recv[r, 3]), True)

    @pl.when(quarter(2))
    def _():
        receive(r, 1)
        new = adjoint(total[r, 0], total[r, 1])
        total[r + 1, 2] = total[r, 2] + new[:, :w]
        total[r + 1, 3] = total[r, 3] + new[:, w:]
        direct(r + 1, 1, core).start()
        near(1).start()
        new = adjoint(right_map[0], right_map[1])
        right_map[2] = right_map[2] + new[:, :w]
        right_map[3] = right_map[3] + new[:, w:]

    @pl.when(quarter(3))
    def _():
        take(r, 0, 0)
        new = product(left_map[0], pair(recv[r, 0], recv[r, 1]))
        left_map[0] = new[:, :w]
        left_map[1] = new[:, w:] + left_map[1]

    z = rounds - 1
    stack = maps[...].reshape(2 * w, w)
    tail = pair(tails[0], tails[1])

    def finish(y):
        rest = y[w:] - product(right_map[2], y[w:]) - right_map[3]
        x = product(tail, rest, True)
        return x[:w], x[w:] + product(inverses[0, 0], y[:w], True)

    def put(x1, x0):
        white[...] = jnp.concatenate([x0, x1], 0).reshape(tx, ty, count)

    @pl.when(last_bit == 0)
    def _():
        x1, x0 = finish(values[...].reshape(2 * w, count) + product(stack, left_map[1]))
        back = product(right_map[0], tail)
        receive(z, 1)
        middle = product(recv[z, 2], total[z, 1]) + recv[z, 3]
        change = product(back, middle, True)
        put(x1 - change[:w], x0 - change[w:])

    @pl.when(last_bit == 1)
    def _():
        new = product(stack, pair(left_map[0], left_map[1]))
        base = values[...].reshape(2 * w, count) + new[:, w:]
        receive(z, 0)
        put(*finish(base + product(new[:, :w], recv[z, 1])))

    out = white[...]
    grad[0] = jnp.sum(out * samples[...], axis=2) * (1.0 / count)
    grad[1] = jnp.sum(out * lap_x[...], axis=2) * (1.0 / count)
    grad[2] = jnp.sum(out * lap_y[...], axis=2) * (1.0 / count)

    for i in range(4):
        @pl.when(neighbours[i][0])
        def _(i=i):
            halos[i].wait_send()
    for m in range(4):
        swap(m).wait_send()
    for r in range(1, rounds - 2):
        for k in range(2):
            give(r, 1, k).wait_send()
            hand(r, 1, k).wait_send()
    r, z = rounds - 2, rounds - 1
    for p, started in enumerate((
        (direct(r, 0, core), hand(r, 1, 0), hand(r, 1, 1)),
        (give(r, 1, 0), give(r, 1, 1), relay(r, 0, core), direct(z, 0, core), near(0)),
        (give(r, 0, 0), relay(r, 1, core), direct(z, 1, core), near(1)),
        (direct(r, 1, core), hand(r, 0, 0)),
    )):
        @pl.when(quarter(p))
        def _(p=p, started=started):
            for one in started + (relay(z, 1 - p // 2, core),):
                one.wait_send()


def body(n_front, n_lat, *arrays):
    samples, inverses = arrays[0], arrays[4]
    tx, ty, count = samples.shape
    w = inverses.shape[-1]
    rounds = n_lat.bit_length() + n_front.bit_length() - 2
    vmem = pl.BlockSpec(memory_space=pltpu.VMEM)
    return pl.pallas_call(
        functools.partial(kernel, n_front, n_lat),
        out_shape=(pltpu.VMEM((tx, ty, count), F32), pltpu.VMEM((3, tx, ty), F32)),
        in_specs=[pl.BlockSpec(memory_space=pltpu.HBM)] * 6,
        out_specs=(vmem, vmem),
        scratch_shapes=[
            *[pltpu.VMEM(a.shape, F32) for a in arrays],
            pltpu.SemaphoreType.DMA((6,)),
            pltpu.VMEM((tx, ty, count), F32),
            pltpu.VMEM((tx, ty, count), F32),
            pltpu.VMEM((2, tx, count), F32),
            pltpu.VMEM((2, ty, count), F32),
            pltpu.VMEM((2, tx, count), F32),
            pltpu.VMEM((2, w, w), F32),
            pltpu.VMEM((2, w, w), F32),
            pltpu.VMEM((2, w, count), F32),
            pltpu.VMEM((4, w, w), F32),
            pltpu.VMEM((2, w, w), F32),
            pltpu.VMEM((rounds, 4, w, w), F32),
            pltpu.VMEM((rounds, 4, w, w), F32),
            pltpu.SemaphoreType.DMA((4,)),
            pltpu.SemaphoreType.DMA((4,)),
            pltpu.SemaphoreType.DMA((rounds, 4)),
            pltpu.SemaphoreType.DMA((rounds, 4)),
        ],
        compiler_params=pltpu.CompilerParams(
            collective_id=0, has_side_effects=True, vmem_limit_bytes=48 * 1024 * 1024),
    )(*[pltpu.with_memory_space_constraint(a, pltpu.HBM) for a in arrays])


def solution(mesh):
    placed = (
        P("front", "lat", None),
        P("front", "lat"),
        P("front", "lat"),
        P("front", "lat"),
        P("front", "lat", None, None),
        P("front", "lat", None, None),
    )
    return jax.shard_map(
        functools.partial(body, mesh.shape["front"], mesh.shape["lat"]),
        mesh=mesh,
        in_specs=placed,
        out_specs=(P("front", "lat", None), P(None, "front", "lat")),
        check_vma=False,
    )
```

```python
import functools
import jax
import jax.numpy as jnp
from jax import lax
from jax.experimental import pallas as pl
from jax.experimental.pallas import tpu as pltpu
from jax.sharding import PartitionSpec as P

MESH = pl.DeviceIdType.MESH
F32 = jnp.float32
BF16 = jnp.bfloat16


def split(value):
    high = value.astype(BF16)
    return high, (value - high.astype(F32)).astype(BF16)


def product(left, right, transposed=False):
    dim = 0 if transposed else 1
    lh, ll = split(left)
    rh, rl = split(right)
    return lax.dot_general(
        jnp.concatenate([lh, ll, lh], axis=dim),
        jnp.concatenate([rh, rh, rl], axis=0),
        (((dim,), (0,)), ((), ())),
        preferred_element_type=F32,
    )


def pair(left, right):
    return jnp.concatenate([left, right], axis=1)


def kernel(n_front, n_lat, samples_in, reaction_in, weight_x_in, weight_y_in, inverses_in, couplings_in,
           white, grad, samples, reaction, weight_x, weight_y, inverses, couplings, loads, lap_x, lap_y, edges, halo_x, halo_y, maps, tails, values, right_map, left_map,
           total, recv, halo_send, halo_recv, sends, recvs):
    front, lat = lax.axis_index("front"), lax.axis_index("lat")
    lat_rounds = n_lat.bit_length() - 1
    rounds = lat_rounds + n_front.bit_length() - 1
    tx, ty, count = samples.shape
    w = inverses.shape[-1]

    def bit_of(r):
        if r < lat_rounds:
            return lax.rem(lax.div(lat, 1 << r), 2)
        return lax.rem(lax.div(front, 1 << (r - lat_rounds)), 2)

    def partner(r):
        sign = 1 - 2 * bit_of(r)
        if r < lat_rounds:
            return (front, lat + sign * (1 << r))
        return (front + sign * (1 << (r - lat_rounds)), lat)

    neighbours = (
        (front < n_front - 1, (front + 1, lat)),
        (front > 0, (front - 1, lat)),
        (lat < n_lat - 1, (front, lat + 1)),
        (lat > 0, (front, lat - 1)),
    )

    inputs = [
        pltpu.make_async_copy(source, here, loads.at[i]) for i, (source, here) in enumerate((
            (samples_in, samples), (reaction_in, reaction), (weight_x_in, weight_x),
            (weight_y_in, weight_y), (inverses_in, inverses), (couplings_in, couplings)))]
    for i in (0, 4, 5, 1, 2, 3):
        inputs[i].start()
    middle_step = 1 - 2 * bit_of(rounds - 1)
    neighbours_all = neighbours + (
        (bit_of(rounds - 2) != bit_of(rounds - 1),
         (front + middle_step * (1 << (rounds - 2 - lat_rounds)), lat)),)
    barrier = pltpu.get_barrier_semaphore()
    for r in range(rounds):
        pl.semaphore_signal(barrier, inc=1, device_id=partner(r), device_id_type=MESH)
    for exists, target in neighbours_all:
        @pl.when(exists)
        def _(target=target):
            pl.semaphore_signal(barrier, inc=1, device_id=target, device_id_type=MESH)

    samples_copy, reaction_copy, weight_x_copy, weight_y_copy, inverses_copy, couplings_copy = inputs
    samples_copy.wait()
    s = samples[...]
    edges[0] = s[:, ty - 1, :]
    edges[1] = s[:, 0, :]
    inverses_copy.wait()
    couplings_copy.wait()
    inv0, inv1 = inverses[0, 0], inverses[0, 1]
    t0 = -product(inv0, couplings[0, 0])
    t1 = -product(inv1, couplings[0, 1])
    maps[0] = t0

    peers = rounds
    for exists, _ in neighbours_all:
        peers = peers + exists.astype(jnp.int32)
    pl.semaphore_wait(barrier, peers)

    halos = []
    for i, (source, landing) in enumerate((
        (samples.at[tx - 1], halo_x.at[0]),
        (samples.at[0], halo_x.at[1]),
        (edges.at[0], halo_y.at[0]),
        (edges.at[1], halo_y.at[1]),
    )):
        halos.append(pltpu.make_async_remote_copy(
            src_ref=source, dst_ref=landing, send_sem=halo_send.at[i], recv_sem=halo_recv.at[i],
            device_id=neighbours[i][1], device_id_type=MESH))

        @pl.when(neighbours[i][0])
        def _(i=i):
            halos[i].start()

    core = bit_of(0)

    def swap(m):
        return pltpu.make_async_remote_copy(
            src_ref=total.at[0, m], dst_ref=recv.at[0, m],
            send_sem=sends.at[0, m], recv_sem=recvs.at[0, m],
            device_id=partner(0), device_id_type=MESH)

    def piece(ref, r, kind, which):
        if kind == 0:
            return ref.at[r, 1, pl.ds(which * (w // 2), w // 2)]
        if kind == 1:
            return ref.at[r, pl.ds(2 + which, 1)]
        return ref.at[r, pl.ds(2 * which, 2)]

    def remote(source, landing, sent, arrived, target):
        return pltpu.make_async_remote_copy(
            src_ref=source, dst_ref=landing, send_sem=sent, recv_sem=arrived,
            device_id=target, device_id_type=MESH)

    def direct(r, kind, which):
        return remote(piece(total, r, kind, which), piece(recv, r, kind, which),
                      sends.at[r, 0], recvs.at[r, which], partner(r))

    def relay(r, kind, which):
        return remote(piece(recv, r, kind, which), piece(recv, r, kind, which),
                      sends.at[r, 2], recvs.at[r, which], partner(0))

    def receive(r, kind):
        direct(r, kind, core).wait_recv()
        relay(r, kind, core).start()
        relay(r, kind, 1 - core).wait_recv()

    def matrix(side, which, k):
        return which + 2 * k if side == 0 else 2 * which + k

    def give(r, side, k, which=core):
        m = matrix(side, which, k)
        return remote(total.at[r, m], recv.at[r, m], sends.at[r, k], recvs.at[r, m], partner(r))

    def hand(r, side, k, which=core):
        m = matrix(side, which, k)
        return remote(recv.at[r, m], recv.at[r, m], sends.at[r, 2 + k], recvs.at[r, m], partner(0))

    first_bit, last_bit = bit_of(rounds - 2), bit_of(rounds - 1)

    def quarter(p):
        return (first_bit == p % 2) & (last_bit == p // 2)

    def near(kind):
        r = rounds - 1
        step = (1 - 2 * kind) * (1 << (rounds - 2 - lat_rounds))
        return remote(piece(total, r, kind, core), piece(recv, r, kind, core),
                      sends.at[r, 1], recvs.at[r, core], (front + step, lat))

    def sent(r, m):
        if r < rounds - 2:
            @pl.when(core == m // 2)
            def _():
                give(r, 1, m % 2, m // 2).start()
            return

        @pl.when(quarter(1) & (core == m // 2))
        def _():
            give(r, 1, m % 2, m // 2).start()

        if m == 1:
            @pl.when(quarter(0))
            def _():
                direct(r, 0, core).start()

        if m < 2:
            @pl.when(quarter(2) & (core == m))
            def _():
                give(r, 0, 0, m).start()
        else:
            @pl.when(quarter(3) & (core == m - 2))
            def _():
                direct(r, 1, m - 2).start()

    def matrices(r, earlier, later):
        start = earlier[r, 0]
        both = product(jnp.concatenate([later[r, 0], later[r, 2]], 0), start)
        total[r + 1, 0] = both[:w]
        sent(r + 1, 0)
        total[r + 1, 2] = earlier[r, 2] + product(start, both[w:], True)
        sent(r + 1, 2)

    def vectors(r, earlier, later):
        both = product(jnp.concatenate([later[r, 0], later[r, 2]], 0), earlier[r, 1])
        total[r + 1, 1] = both[:w] + later[r, 1]
        sent(r + 1, 1)
        total[r + 1, 3] = earlier[r, 3] + product(earlier[r, 0], both[w:] + later[r, 3], True)
        sent(r + 1, 3)

    def merge(step, r):
        @pl.when(bit_of(r) == 0)
        def _():
            step(r, total, recv)

        @pl.when(bit_of(r) == 1)
        def _():
            step(r, recv, total)

    full = product(t1, t0)
    maps[1] = full
    total[0, 0] = full
    swap(0).start()
    stack = maps[0:2].reshape(2 * w, w)
    total[0, 2] = -product(stack, stack, True)
    swap(2).start()
    tail = product(t1, inv0)
    tails[0] = inv1
    tails[1] = tail

    swap(0).wait_recv()
    swap(2).wait_recv()
    merge(matrices, 0)
    for i, landing in enumerate((halo_x.at[0], halo_x.at[1], halo_y.at[0], halo_y.at[1])):
        comes = neighbours[i ^ 1][0]

        @pl.when(comes)
        def _(i=i):
            halos[i].wait_recv()

        @pl.when(jnp.logical_not(comes))
        def _(landing=landing):
            landing[...] = jnp.zeros((landing.shape[0], count), F32)

    reaction_copy.wait()
    weight_x_copy.wait()
    weight_y_copy.wait()
    hx, hy = halo_x[...], halo_y[...]
    lx = 2.0 * s - jnp.concatenate([hx[0:1], s[:-1]], 0) - jnp.concatenate([s[1:], hx[1:2]], 0)
    ly = 2.0 * s - jnp.concatenate([hy[0][:, None, :], s[:, :-1]], 1) - jnp.concatenate([s[:, 1:], hy[1][:, None, :]], 1)
    lap_x[...] = lx
    lap_y[...] = ly
    resid = (reaction[...][:, :, None] * s + weight_x[...][:, :, None] * lx
             + weight_y[...][:, :, None] * ly).reshape(2 * w, count)
    y0 = product(inv0, resid[:w])
    y1 = product(pair(tail, inv1), resid)
    values[0] = y0
    values[1] = y1
    total[0, 1] = y1
    swap(1).start()
    total[0, 3] = -product(stack, jnp.concatenate([y0, y1], 0), True)
    swap(3).start()
    swap(1).wait_recv()
    swap(3).wait_recv()
    merge(vectors, 0)
    eye = (lax.broadcasted_iota(jnp.int32, (w, w), 0) == lax.broadcasted_iota(jnp.int32, (w, w), 1)).astype(F32)
    zero = jnp.zeros((w, w), F32)

    @pl.when(core == 0)
    def _():
        right_map[...] = recv[0]
        left_map[0] = eye
        left_map[1] = zero

    @pl.when(core == 1)
    def _():
        left_map[...] = recv[0, 0:2]
        right_map[0] = eye
        right_map[1] = zero
        right_map[2] = zero
        right_map[3] = zero

    def extend_right(other):
        start = right_map[0]
        ab = pair(start, right_map[1])
        both = product(jnp.concatenate([other[0], other[2]], 0), ab)
        right_map[0] = both[:w, :w]
        right_map[1] = both[:w, w:] + other[1]
        new = product(start, pair(both[w:, :w], both[w:, w:] + other[3]), True)
        right_map[2] = right_map[2] + new[:, :w]
        right_map[3] = right_map[3] + new[:, w:]

    def take(r, side, k):
        give(r, side, k).wait_recv()
        hand(r, side, k).start()
        hand(r, side, k, 1 - core).wait_recv()

    for r in range(1, rounds - 2):
        take(r, 1, 0)
        merge(matrices, r)
        take(r, 1, 1)
        merge(vectors, r)

        @pl.when(bit_of(r) == 0)
        def _(r=r):
            extend_right(recv.at[r])

        @pl.when(bit_of(r) == 1)
        def _(r=r):
            new = product(left_map[0], pair(recv[r, 0], recv[r, 1]))
            left_map[0] = new[:, :w]
            left_map[1] = new[:, w:] + left_map[1]

    r = rounds - 2

    @pl.when(quarter(0))
    def _():
        take(r, 1, 0)
        take(r, 1, 1)
        total[r + 1, 1] = product(recv[r, 0], total[r, 1]) + recv[r, 1]
        extend_right(recv.at[r])

    @pl.when(quarter(1))
    def _():
        receive(r, 0)
        total[r + 1, 1] = product(total[r, 0], recv[r, 1]) + total[r, 1]
        direct(r + 1, 0, core).start()
        near(0).start()
        left_map[1] = product(left_map[0], recv[r, 1]) + left_map[1]

    def adjoint(a, b):
        mid = product(recv[r, 2], pair(a, b))
        return product(a, pair(mid[:, :w], mid[:, w:] + recv[r, 3]), True)

    def one(r, which):
        @pl.when(core == which)
        def _():
            direct(r, 1, which).wait_recv()
            relay(r, 1, which).start()

        @pl.when(core != which)
        def _():
            relay(r, 1, which).wait_recv()

    def give_back(which):
        @pl.when(core == which)
        def _():
            direct(rounds - 1, 1, which).start()
            near(1).start()

    @pl.when(quarter(2))
    def _():
        one(r, 0)
        mid = product(recv[r, 2], pair(total[r, 0], total[r, 1]))
        total[r + 1, 2] = total[r, 2] + product(total[r, 0], mid[:, :w], True)
        give_back(0)
        one(r, 1)
        total[r + 1, 3] = total[r, 3] + product(total[r, 0], mid[:, w:] + recv[r, 3], True)
        give_back(1)
        new = adjoint(right_map[0], right_map[1])
        right_map[2] = right_map[2] + new[:, :w]
        right_map[3] = right_map[3] + new[:, w:]

    @pl.when(quarter(3))
    def _():
        take(r, 0, 0)
        new = product(left_map[0], pair(recv[r, 0], recv[r, 1]))
        left_map[0] = new[:, :w]
        left_map[1] = new[:, w:] + left_map[1]

    z = rounds - 1
    stack = maps[...].reshape(2 * w, w)
    tail = pair(tails[0], tails[1])

    def finish(y):
        rest = y[w:] - product(right_map[2], y[w:]) - right_map[3]
        x = product(tail, rest, True)
        return x[:w], x[w:] + product(inverses[0, 0], y[:w], True)

    def put(x1, x0):
        white[...] = jnp.concatenate([x0, x1], 0).reshape(tx, ty, count)

    @pl.when(last_bit == 0)
    def _():
        x1, x0 = finish(values[...].reshape(2 * w, count) + product(stack, left_map[1]))
        back = product(right_map[0], tail)
        one(z, 0)
        middle = product(recv[z, 2], total[z, 1])
        one(z, 1)
        middle = middle + recv[z, 3]
        change = product(back, middle, True)
        put(x1 - change[:w], x0 - change[w:])

    @pl.when(last_bit == 1)
    def _():
        new = product(stack, pair(left_map[0], left_map[1]))
        base = values[...].reshape(2 * w, count) + new[:, w:]
        receive(z, 0)
        put(*finish(base + product(new[:, :w], recv[z, 1])))

    out = white[...]
    grad[0] = jnp.sum(out * samples[...], axis=2) * (1.0 / count)
    grad[1] = jnp.sum(out * lap_x[...], axis=2) * (1.0 / count)
    grad[2] = jnp.sum(out * lap_y[...], axis=2) * (1.0 / count)

    for i in range(4):
        @pl.when(neighbours[i][0])
        def _(i=i):
            halos[i].wait_send()
    for m in range(4):
        swap(m).wait_send()
    for r in range(1, rounds - 2):
        for k in range(2):
            give(r, 1, k).wait_send()
            hand(r, 1, k).wait_send()
    r, z = rounds - 2, rounds - 1
    for p, started in enumerate((
        (direct(r, 0, core), hand(r, 1, 0), hand(r, 1, 1)),
        (give(r, 1, 0), give(r, 1, 1), relay(r, 0, core), direct(z, 0, core), near(0)),
        (give(r, 0, 0), relay(r, 1, core), direct(z, 1, core), near(1)),
        (direct(r, 1, core), hand(r, 0, 0)),
    )):
        @pl.when(quarter(p))
        def _(p=p, started=started):
            for one in started + (relay(z, 1 - p // 2, core),):
                one.wait_send()


def body(n_front, n_lat, *arrays):
    samples, inverses = arrays[0], arrays[4]
    tx, ty, count = samples.shape
    w = inverses.shape[-1]
    rounds = n_lat.bit_length() + n_front.bit_length() - 2
    vmem = pl.BlockSpec(memory_space=pltpu.VMEM)
    return pl.pallas_call(
        functools.partial(kernel, n_front, n_lat),
        out_shape=(pltpu.VMEM((tx, ty, count), F32), pltpu.VMEM((3, tx, ty), F32)),
        in_specs=[pl.BlockSpec(memory_space=pltpu.HBM)] * 6,
        out_specs=(vmem, vmem),
        scratch_shapes=[
            *[pltpu.VMEM(a.shape, F32) for a in arrays],
            pltpu.SemaphoreType.DMA((6,)),
            pltpu.VMEM((tx, ty, count), F32),
            pltpu.VMEM((tx, ty, count), F32),
            pltpu.VMEM((2, tx, count), F32),
            pltpu.VMEM((2, ty, count), F32),
            pltpu.VMEM((2, tx, count), F32),
            pltpu.VMEM((2, w, w), F32),
            pltpu.VMEM((2, w, w), F32),
            pltpu.VMEM((2, w, count), F32),
            pltpu.VMEM((4, w, w), F32),
            pltpu.VMEM((2, w, w), F32),
            pltpu.VMEM((rounds, 4, w, w), F32),
            pltpu.VMEM((rounds, 4, w, w), F32),
            pltpu.SemaphoreType.DMA((4,)),
            pltpu.SemaphoreType.DMA((4,)),
            pltpu.SemaphoreType.DMA((rounds, 4)),
            pltpu.SemaphoreType.DMA((rounds, 4)),
        ],
        compiler_params=pltpu.CompilerParams(
            collective_id=0, has_side_effects=True, vmem_limit_bytes=48 * 1024 * 1024),
    )(*[pltpu.with_memory_space_constraint(a, pltpu.HBM) for a in arrays])


def solution(mesh):
    placed = (
        P("front", "lat", None),
        P("front", "lat"),
        P("front", "lat"),
        P("front", "lat"),
        P("front", "lat", None, None),
        P("front", "lat", None, None),
    )
    return jax.shard_map(
        functools.partial(body, mesh.shape["front"], mesh.shape["lat"]),
        mesh=mesh,
        in_specs=placed,
        out_specs=(P("front", "lat", None), P(None, "front", "lat")),
        check_vma=False,
    )
```
